256 devices in a mesh: brick: 16 (over y_lo, z), depth: 16 (over x, y_hi, core).
Axes of the slice: x: 4, y: 4 (y_hi: 2, y_lo: 2; y = y_hi * 2 + y_lo), z: 8, core: 2. Of those that a mesh axis runs over, the one named last changes fastest.
Arguments:
- conductivity: float32 [128, 256, 256], P('brick', 'depth'), may hold values from 0.03 to 10.5, as said below
- initial_field: float32 [2, 128, 256, 256], P(None, 'brick', 'depth'), may hold values from -1.2 to 1.2
- adjoint_initial: float32 [2, 128, 256, 256], P(None, 'brick', 'depth'), may hold values from -0.36 to 0.36
- src_cell: int32 [16, 16, 64], P('brick', 'depth'), may hold values from 0 to 32767
- src_amp: float32 [16, 16, 2, 64], P('brick', 'depth'), may hold values from -24 to 24
- rec_cell: int32 [16, 16, 64], P('brick', 'depth'), may hold values from 0 to 32767
- observed: float32 [16, 16, 2, 64], P('brick', 'depth'), may hold values from -12 to 12
- cov_blocks: bfloat16 [16, 16, 16, 512, 512], P('brick', 'depth'), may hold values from -0.25 to 0.25
- cov_rows: int32 [16, 16, 16], P('brick', 'depth'), may hold values from 0 to 63
- cov_cols: int32 [16, 16, 16], P('brick', 'depth'), may hold values from 0 to 1023
Outputs:
- forward: float32 [2, 128, 256, 256], P(None, 'brick', 'depth')
- preconditioned: float32 [128, 256, 256], P('brick', 'depth')
The draws below stay inside these ranges and needn't reach their ends.
Inputs may be any that keep to these rules, and one draw needn't show every extreme that they name: `conductivity`: positive everywhere.
All inputs are finite; a program needn't handle non-finite values.
Results may differ from the reference program's by a relative error of at most 0.0032.
Values may be sent and summed in bfloat16 or wider, within the bound.
A program may use at most 128 MiB of HBM per device.

```python
import math
import jax
import jax.numpy as jnp
from jax import lax

CX = 8
CZ = 16
NY = 256
FREQS = 2
ITERS = 3
BLOCK = 512
NNZ = 16
NS = 64
NR = 64
NX = 128
NZ = 256
BLK_DEV = 64
COL_BLOCKS = 1024
N_BRICK = 16
N_DEPTH = 16


def coordinates():
    x_frac = ((jnp.arange(NX, dtype=jnp.float32) + 0.5) / NX)[:, None, None]
    z_frac = ((jnp.arange(NZ, dtype=jnp.float32) + 0.5) / NZ)[None, :, None]
    y_frac = ((jnp.arange(NY, dtype=jnp.float32) + 0.5) / NY)[None, None, :]
    return (x_frac, z_frac, y_frac)


def draw_conductivity(key, part):
    own_key = jax.random.fold_in(key, 5)
    x_frac, z_frac, y_frac = coordinates()
    trend = jnp.exp((0.4 - 1.5 * z_frac + 0.3 * x_frac) * math.log(10.0))
    rough = jnp.exp(jax.random.uniform(own_key, (NX, NZ, NY), jnp.float32, -math.log(2.0), math.log(2.0)))
    return trend * rough


def field_draw(key, magnitude):
    key_phase, key_rough = jax.random.split(key)
    x_frac, z_frac, y_frac = coordinates()
    x_frac = x_frac[None]
    z_frac = z_frac[None]
    y_frac = y_frac[None]
    freq = jnp.arange(FREQS, dtype=jnp.float32)[:, None, None, None]
    phases = jax.random.uniform(key_phase, (3, FREQS, 1, 1, 1), jnp.float32, 0.0, 1.0)
    two_pi = 2.0 * math.pi
    smooth = jnp.sin(two_pi * (2.0 * x_frac + phases[0])) * jnp.sin(two_pi * (1.5 * z_frac + phases[1])) * jnp.cos(two_pi * (3.0 * y_frac + phases[2]))
    shape = (FREQS, NX, NZ, NY)
    envelope = jnp.exp((0.3 * x_frac - (0.5 + 0.3 * freq) * z_frac) * math.log(10.0))
    rough = 0.7 * jax.random.truncated_normal(key_rough, -4.0, 4.0, shape, jnp.float32)
    return magnitude * envelope * (0.8 * smooth + rough)


def draw_initial_field(key, part):
    return field_draw(jax.random.fold_in(key, 11), 0.1)


def draw_adjoint_initial(key, part):
    return field_draw(jax.random.fold_in(key, 23), 0.03)


def touch_ends(entries, rng, low, high):
    longest = entries.shape.index(max(entries.shape))
    spots = []
    for shift in (0, 1):
        where = [jax.random.randint(jax.random.fold_in(rng, axis), (), 0, length) for axis, length in enumerate(entries.shape)]
        where[longest] = (where[longest] + shift) % entries.shape[longest]
        spots.append(tuple(where))
    return entries.at[spots[0]].set(low).at[spots[1]].set(high)


def block_levels(rng, dims, cuts, smallest, high):
    gain = 1.0
    for position, parts in cuts:
        heights = jax.random.uniform(jax.random.fold_in(jax.random.fold_in(rng, 6), position), (parts,), jnp.float32, smallest / len(cuts), high / len(cuts))
        gain = gain * jnp.repeat(jnp.exp(heights), dims[position] // parts).reshape((-1,) + (1,) * (len(dims) - 1 - position))
    return gain


def scatter_about(stream_key, shape, width, bound, cuts=(), kind=jnp.bfloat16):
    drawn = width * jax.random.normal(stream_key, shape, jnp.float32)
    if cuts:
        drawn = drawn * block_levels(stream_key, shape, cuts, -0.22, 0.18)
    return jnp.clip(drawn, -bound, bound).astype(kind)


def setup_inputs(seed: int = 0) -> dict:
    splits = jax.random.split(jax.random.key(seed), 11)
    conductivity = draw_conductivity(jax.random.fold_in(splits[10], 71), 0)
    initial_field = draw_initial_field(jax.random.fold_in(splits[10], 71), 0)
    adjoint_initial = draw_adjoint_initial(jax.random.fold_in(splits[10], 71), 0)
    src_cell = touch_ends(jax.random.randint(splits[3], (N_BRICK, N_DEPTH, NS), 0, CX * CZ * NY), jax.random.fold_in(splits[3], 1), 0, (CX * CZ * NY) - 1).astype(jnp.int32)
    src_amp = scatter_about(splits[4], (N_BRICK, N_DEPTH, FREQS, NS), 4.0, 24.0, ((0, 16), (1, 16)), jnp.float32)
    rec_cell = touch_ends(jax.random.randint(splits[5], (N_BRICK, N_DEPTH, NR), 0, CX * CZ * NY), jax.random.fold_in(splits[5], 1), 0, (CX * CZ * NY) - 1).astype(jnp.int32)
    observed = scatter_about(splits[6], (N_BRICK, N_DEPTH, FREQS, NR), 2.0, 12.0, ((0, 16), (1, 16)), jnp.float32)
    cov_blocks = scatter_about(splits[7], (N_BRICK, N_DEPTH, NNZ, BLOCK, BLOCK), BLOCK ** -0.5, 0.25, ((0, 16), (1, 16)))
    cov_rows = touch_ends(jax.random.randint(splits[8], (N_BRICK, N_DEPTH, NNZ), 0, BLK_DEV), jax.random.fold_in(splits[8], 1), 0, BLK_DEV - 1).astype(jnp.int32)
    cov_cols = touch_ends(jax.random.randint(splits[9], (N_BRICK, N_DEPTH, NNZ), 0, COL_BLOCKS), jax.random.fold_in(splits[9], 1), 0, COL_BLOCKS - 1).astype(jnp.int32)
    return dict(conductivity=conductivity, initial_field=initial_field, adjoint_initial=adjoint_initial, src_cell=src_cell, src_amp=src_amp, rec_cell=rec_cell, observed=observed, cov_blocks=cov_blocks, cov_rows=cov_rows, cov_cols=cov_cols)


LAPLACE_SHIFTS = (0.5, 2.0)


def to_local(volume):
    leading = volume.shape[:-3]
    pieces = volume.reshape(leading + (N_BRICK, CX, N_DEPTH, CZ, NY))
    pieces = jnp.swapaxes(pieces, -4, -3)
    return pieces.reshape(leading + (N_BRICK, N_DEPTH, CX * CZ * NY))


def from_local(flat_cells):
    leading = flat_cells.shape[:-3]
    pieces = flat_cells.reshape(leading + (N_BRICK, N_DEPTH, CX, CZ, NY))
    pieces = jnp.swapaxes(pieces, -4, -3)
    return pieces.reshape(leading + (N_BRICK * CX, N_DEPTH * CZ, NY))


def spread(values):
    return values[:, None, None, None]


def operate(volume, damping):
    padded = jnp.pad(volume, ((0, 0), (1, 1), (1, 1), (1, 1)))
    beside = padded[:, 2:, 1:-1, 1:-1] + padded[:, :-2, 1:-1, 1:-1]
    beside = beside + padded[:, 1:-1, 2:, 1:-1] + padded[:, 1:-1, :-2, 1:-1]
    beside = beside + padded[:, 1:-1, 1:-1, 2:] + padded[:, 1:-1, 1:-1, :-2]
    return (6.0 + damping) * volume - beside


def conjugate(source_term, initial, damping):
    solution = initial
    residual = source_term - operate(initial, damping)
    direction = residual
    norm_now = jnp.sum(residual * residual, axis=(1, 2, 3))
    for iteration in range(ITERS):
        applied = operate(direction, damping)
        step_len = norm_now / jnp.sum(direction * applied, axis=(1, 2, 3))
        solution = solution + spread(step_len) * direction
        residual = residual - spread(step_len) * applied
        if iteration + 1 < ITERS:
            norm_next = jnp.sum(residual * residual, axis=(1, 2, 3))
            direction = residual + spread(norm_next / norm_now) * direction
            norm_now = norm_next
    return solution


def place_points(cells, amounts):
    def one_device(cell_list, amount_list):
        return jnp.zeros((2, CX * CZ * NY), jnp.float32).at[:, cell_list].add(amount_list)

    placed = jax.vmap(jax.vmap(one_device))(cells, amounts)
    return from_local(jnp.moveaxis(placed, 2, 0))


def read_points(volume, cells):
    local_cells = jnp.moveaxis(to_local(volume), 0, 2)

    def one_device(values_here, cell_list):
        return values_here[:, cell_list]

    return jax.vmap(jax.vmap(one_device))(local_cells, cells)


def reference(conductivity, initial_field, adjoint_initial, src_cell, src_amp, rec_cell, observed, cov_blocks, cov_rows, cov_cols):
    shifts = jnp.array(LAPLACE_SHIFTS, jnp.float32)
    damping = spread(shifts) * conductivity[None]
    forward = conjugate(place_points(src_cell, src_amp), initial_field, damping)
    misfit = read_points(forward, rec_cell) - observed
    adjoint = conjugate(place_points(rec_cell, misfit), adjoint_initial, damping)
    gradient = (-jnp.sum(spread(shifts) * forward * adjoint, axis=0)).astype(jnp.bfloat16)
    blocks_dev = CX * CZ * NY // BLOCK
    grad_blocks = to_local(gradient).reshape(N_BRICK, N_DEPTH * blocks_dev, BLOCK)

    def per_brick(operands):
        brick_grad, brick_blocks, brick_rows, brick_cols = operands
        picked = brick_grad[brick_cols]
        terms = jnp.einsum("dkij,dkj->dki", brick_blocks.astype(jnp.float32), picked.astype(jnp.float32), precision=lax.Precision.HIGHEST)
        targets = jnp.arange(N_DEPTH, dtype=jnp.int32)[:, None] * blocks_dev + brick_rows
        return jnp.zeros((N_DEPTH * blocks_dev, BLOCK), jnp.float32).at[targets].add(terms)

    added = lax.map(per_brick, (grad_blocks, cov_blocks, cov_rows, cov_cols))
    combined = grad_blocks.astype(jnp.float32) + added
    preconditioned = from_local(combined.reshape(N_BRICK, N_DEPTH, CX * CZ * NY))
    return forward, preconditioned
```

```python
import functools

import jax
import jax.numpy as jnp
from jax import lax
from jax.experimental import pallas as pl
from jax.experimental.pallas import tpu as pltpu
from jax.sharding import PartitionSpec as P

LAPLACE_SHIFTS = (0.5, 2.0)
CENTRE = (6.5, 8.0)
ITERS = 3
NB = 16
CX, CZ, NY = 8, 16, 256
HX, HZ = 6, 8
EX, EZ = CX + 2 * HX, CZ + 2 * HZ
NNZ, BLOCK = 16, 512
ROWS = CX * CZ
F32, BF16 = jnp.float32, jnp.bfloat16
MESH = pl.DeviceIdType.MESH
OWN_X, OWN_Z = pl.ds(HX, CX), pl.ds(HZ, CZ)

FACES_X = ((1, 0), (-1, 0))
FACES_Z = ((0, 1), (0, -1))
CORNERS = ((1, 1), (1, -1), (-1, 1), (-1, -1))
AROUND = FACES_X + FACES_Z + CORNERS


def iota(shape, dim):
    return lax.broadcasted_iota(jnp.int32, shape, dim)


def send_x(dx, width, skip=0):
    return pl.ds(HX + CX - skip - width, width) if dx > 0 else pl.ds(HX + skip, width)


def send_z(dz):
    return pl.ds(HZ + CZ - HZ, HZ) if dz > 0 else pl.ds(HZ, HZ)


def land_x(dx, width, skip=0):
    return pl.ds(HX - skip - width, width) if dx > 0 else pl.ds(HX + CX + skip, width)


def land_z(dz):
    return pl.ds(0, HZ) if dz > 0 else pl.ds(HZ + CZ, HZ)


def layer_at(dx, distance, land):
    if land:
        return HX - distance if dx > 0 else HX + CX + distance - 1
    return HX + CX - distance if dx > 0 else HX + distance - 1


def halves(first, second, dz):
    near = (iota((8, 1), 0) >= 4) if dz > 0 else (iota((8, 1), 0) < 4)
    return jnp.where(near, first, pltpu.roll(second, 4, 0))


def pack_face(field, dz):
    slabs = []
    for m in range(CX // 2):
        tiles = [halves(field[f][2 * m], field[f][2 * m + 1], dz) for f in range(2)]
        slabs.append(jnp.concatenate(tiles, axis=0).astype(BF16))
    return slabs


def pack_corner(field, near, zs, dz):
    tiles = [halves(field[f, near[0], zs, :], field[f, near[1], zs, :], dz) for f in range(2)]
    return tiles + [halves(field[0, near[2], zs, :], field[1, near[2], zs, :], dz)]


def cg_coefficients(nu, centre):
    def inner(p, q, shift):
        total = None
        for i, pi in enumerate(p):
            for j, qj in enumerate(q):
                term = pi * qj * nu[i + j + shift]
                total = term if total is None else total + term
        return total

    one = jnp.ones_like(nu[0])
    r, p = [one], [one]
    rr = nu[0]
    x = [jnp.zeros_like(one)] * ITERS
    for it in range(ITERS):
        step = rr / (inner(p, p, 1) + centre * inner(p, p, 0))
        for i, pi in enumerate(p):
            x[i] = x[i] + step * pi
        if it + 1 < ITERS:
            ap = [centre * pi for pi in p] + [jnp.zeros_like(one)]
            for i, pi in enumerate(p):
                ap[i + 1] = ap[i + 1] + pi
            r = r + [jnp.zeros_like(one)]
            r = [ri - step * ai for ri, ai in zip(r, ap)]
            new = inner(r, r, 0)
            beta = new / rr
            p = p + [jnp.zeros_like(one)]
            p = [ri + beta * pi for ri, pi in zip(r, p)]
            rr = new
    return x


def kernel(
    cond_in, x0_in, a0_in, src_in, amp_in, rec_in, obs_in, cov_in, rows_in, cols_in,
    fwd_out, pre_out,
    src_v, amp_v, rec_v, obs_v, rows_v, cols_v, aux, cov, ce, x0e, a0e, mask, srce, obse, cnte, v0, v1, v2, w, fwd, grad, pre, pick_hot,
    sx, rx, sz, rz, sc, rc, ax, bx, az, bz, ac, bc,
    rlist, seen, rseen, rec_hit, rec_y, cols, asum, rsum, psend, precv,
    in_sem, cov_sem, out_sem, list_sem, cols_sem, halo_sem, adj_sem, seen_sem, sum_sem, pick_sem,
):
    b, d = lax.axis_index("brick"), lax.axis_index("depth")

    def at(dx, dz):
        return lax.rem(b + dx + NB, NB), lax.rem(d + dz + NB, NB)

    barrier = pltpu.get_barrier_semaphore()
    for dx, dz in CORNERS:
        pl.semaphore_signal(barrier, inc=1, device_id=at(dx, dz), device_id_type=MESH)

    def greet(o, _):
        pl.semaphore_signal(barrier, inc=1, device_id=at(0, o), device_id_type=MESH)
        pl.semaphore_signal(barrier, inc=1, device_id=at(o, 0), device_id_type=MESH)
        return 0

    lax.fori_loop(1, NB, greet, 0)

    loads = [
        pltpu.make_async_copy(x0_in, x0e.at[:, OWN_X, OWN_Z, :], in_sem.at[0]),
        pltpu.make_async_copy(cond_in, ce.at[OWN_X, OWN_Z, :], in_sem.at[1]),
        pltpu.make_async_copy(src_in, src_v, in_sem.at[2]),
        pltpu.make_async_copy(amp_in, amp_v, in_sem.at[3]),
        pltpu.make_async_copy(rec_in, rec_v, in_sem.at[4]),
        pltpu.make_async_copy(obs_in, obs_v, in_sem.at[5]),
        pltpu.make_async_copy(rows_in, rows_v, in_sem.at[6]),
        pltpu.make_async_copy(cols_in, cols_v, in_sem.at[7]),
        pltpu.make_async_copy(a0_in, a0e.at[:, OWN_X, OWN_Z, :], in_sem.at[8]),
    ]
    for load in loads:
        load.start()
    cov_load = pltpu.make_async_copy(cov_in, cov, cov_sem)
    cov_load.start()

    for load in loads[:2]:
        load.wait()
    for i, (dx, _) in enumerate(FACES_X):
        for f in range(2):
            sx[i, pl.ds(4 * f, 4)] = x0e[f, send_x(dx, 4), OWN_Z, :].astype(BF16)
        sx[i, pl.ds(8, 3)] = ce[send_x(dx, 3), OWN_Z, :].astype(BF16)
    for i, (_, dz) in enumerate(FACES_Z):
        zs = send_z(dz)
        for m, slab in enumerate(pack_face([x0e[f, OWN_X, zs, :] for f in range(2)], dz)):
            sz[i, m] = slab
        for m in range(2):
            tiles = [halves(ce[HX + k, zs, :], ce[HX + k + 1, zs, :], dz) for k in (4 * m, 4 * m + 2)]
            sz[i, 4 + m] = jnp.concatenate(tiles, axis=0).astype(BF16)
    for i, (dx, dz) in enumerate(CORNERS):
        zs = send_z(dz)
        near = [layer_at(dx, k, False) for k in (1, 2, 3)]
        tiles = pack_corner(x0e, near, zs, dz)
        tiles.append(halves(ce[near[0], zs, :], ce[near[1], zs, :], dz))
        sc[i, 0] = jnp.concatenate(tiles[:2], axis=0).astype(BF16)
        sc[i, 1] = jnp.concatenate(tiles[2:], axis=0).astype(BF16)

    for load in loads[2:8]:
        load.wait()

    def twice(row):
        return jnp.concatenate([row, row], axis=1)

    src_cell, rec_cell = src_v[0], rec_v[0]
    aux[0:1, :] = twice((src_cell >> 8).astype(F32))
    aux[1:2, :] = twice((src_cell & (NY - 1)).astype(F32))
    aux[2:4, :] = twice(amp_v[0, 0])
    aux[4:5, :] = twice((rec_cell >> 8).astype(F32))
    aux[5:6, :] = twice((rec_cell & (NY - 1)).astype(F32))
    aux[6:7, :] = jnp.where(iota((1, 128), 1) < 64, 1.0, 0.0)
    aux[7:9, :] = twice(obs_v[0, 0])
    aux[9:16, :] = jnp.zeros((7, 128), F32)
    col_row = jnp.where(iota((NNZ, NNZ), 0) == iota((NNZ, NNZ), 1), cols_v[0].astype(F32), 0.0)
    aux[16:32, :] = jnp.broadcast_to(jnp.sum(col_row, axis=1, keepdims=True), (NNZ, 128))

    pl.semaphore_wait(barrier, 2 * (NB - 1) + len(CORNERS))

    for n, (dx, dz) in enumerate(AROUND):
        pltpu.make_async_remote_copy(
            src_ref=aux.at[pl.ds(0, 16)], dst_ref=rlist.at[n], send_sem=list_sem.at[0], recv_sem=list_sem.at[1],
            device_id=at(dx, dz), device_id_type=MESH).start()

    def exchange(n, dx, dz, src, dst, sems):
        return pltpu.make_async_remote_copy(
            src_ref=src, dst_ref=dst, send_sem=sems.at[n, 0], recv_sem=sems.at[n, 1],
            device_id=at(dx, dz), device_id_type=MESH)

    halos = []
    for group, s, r in ((FACES_X, sx, rx), (FACES_Z, sz, rz), (CORNERS, sc, rc)):
        for i, (dx, dz) in enumerate(group):
            halos.append(exchange(len(halos), dx, dz, s.at[i], r.at[i], halo_sem))
    for copy in halos:
        copy.start()

    def inside(dx, dz):
        bx_, dz_ = b + dx, d + dz
        ok = (bx_ >= 0) & (bx_ < NB) & (dz_ >= 0) & (dz_ < NB)
        return jnp.where(ok, 1.0, 0.0).astype(F32)

    for i, (dx, dz) in enumerate(((0, 0),) + AROUND):
        xs = pl.ds(HX, CX) if dx == 0 else land_x(-dx, HX)
        zs = pl.ds(HZ, CZ) if dz == 0 else land_z(-dz)
        nx, nz = (CX if dx == 0 else HX), (CZ if dz == 0 else HZ)
        mask[xs, zs, :] = jnp.full((nx, nz, NY), inside(dx, dz), F32)

    for zs in (pl.ds(0, HZ), pl.ds(HZ + CZ, HZ)):
        for xs in (pl.ds(0, 3), pl.ds(EX - 3, 3)):
            x0e[:, xs, zs, :] = jnp.zeros((2, 3, HZ, NY), F32)
            a0e[:, xs, zs, :] = jnp.zeros((2, 3, HZ, NY), F32)
        for xs in (pl.ds(0, 4), pl.ds(EX - 4, 4)):
            ce[xs, zs, :] = jnp.zeros((4, HZ, NY), F32)

    lane = iota((1, 128), 1)

    def parts(row, ok):
        value = row * ok
        head = value.astype(BF16).astype(F32)
        return jnp.where(lane < 64, head, value - head)

    def where_points(table, base, dx, dz, width):
        xs = pl.ds(HX, CX) if dx == 0 else land_x(-dx, width)
        zs = pl.ds(HZ, CZ) if dz == 0 else land_z(-dz)
        nx, x_low = (CX, 0) if dx == 0 else ((width, 0) if dx > 0 else (width, CX - width))
        nz, z_low = (CZ, 0) if dz == 0 else ((HZ, 0) if dz > 0 else (HZ, CZ - HZ))
        shape = (nx, nz, 128)
        cell_row = ((iota(shape, 0) + x_low) * CZ + iota(shape, 1) + z_low).reshape(nx * nz, 128).astype(F32)
        hit = cell_row == table[base:base + 1, :]
        along_y = (iota((NY, 128), 0).astype(F32) == table[base + 1:base + 2, :]).astype(F32).astype(BF16)
        return hit, along_y, xs, zs, (nx, nz)

    def place(hit, along_y, rows, shape):
        left = jnp.concatenate([jnp.where(hit, row, 0.0).astype(BF16) for row in rows], axis=0)
        placed = lax.dot_general(left, along_y, (((1,), (1,)), ((), ())), preferred_element_type=F32)
        return placed.reshape((len(rows),) + shape + (NY,))

    def place_sources(table, dx, dz):
        ok = inside(dx, dz)
        hit, along_y, xs, zs, shape = where_points(table, 0, dx, dz, 3)
        srce[:, xs, zs, :] = place(hit, along_y, [parts(table[2 + f:3 + f, :], ok) for f in range(2)], shape)

    def place_own_receivers():
        rows = [own_table[6:7, :]] + [parts(own_table[7 + f:8 + f, :], 1.0) for f in range(2)]
        placed = place(*own_points[:2], rows, own_points[4])
        cnte[...] = placed[0]
        obse[...] = placed[1:3]

    own_table = aux[0:16, :]
    place_sources(own_table, 0, 0)

    loads[8].wait()
    for i, (dx, _) in enumerate(FACES_X):
        for f in range(2):
            ax[i, pl.ds(4 * f, 4)] = a0e[f, send_x(dx, 4), OWN_Z, :].astype(BF16)
    for i, (_, dz) in enumerate(FACES_Z):
        for m, slab in enumerate(pack_face([a0e[f, OWN_X, send_z(dz), :] for f in range(2)], dz)):
            az[i, m] = slab
    for i, (dx, dz) in enumerate(CORNERS):
        tiles = pack_corner(a0e, [layer_at(dx, k, False) for k in (1, 2, 3)], send_z(dz), dz)
        ac[i, 0] = jnp.concatenate(tiles[:2], axis=0).astype(BF16)
        ac[i, 1] = jnp.concatenate([tiles[2], tiles[2]], axis=0).astype(BF16)
    adjoint_halos = []
    for group, s, r in ((FACES_X, ax, bx), (FACES_Z, az, bz), (CORNERS, ac, bc)):
        for i, (dx, dz) in enumerate(group):
            adjoint_halos.append(exchange(len(adjoint_halos), dx, dz, s.at[i], r.at[i], adj_sem))

    lists = pltpu.make_async_remote_copy(
        src_ref=rlist, dst_ref=rlist, send_sem=list_sem.at[0], recv_sem=list_sem.at[1],
        device_id=at(1, 0), device_id_type=MESH)
    lists.wait_recv()
    for n, (dx, dz) in enumerate(AROUND):
        place_sources(rlist[n], -dx, -dz)
    for copy in adjoint_halos:
        copy.start()

    def unpack_face(message, field, zs, ok):
        for m in range(CX // 2):
            slab = message[m].astype(F32) * ok
            for f in range(2):
                tile = slab[8 * f:8 * f + 8]
                field[f, HX + 2 * m, zs, :] = tile
                field[f, HX + 2 * m + 1, zs, :] = pltpu.roll(tile, 4, 0)

    def unpack_corner(message, field, near, zs, ok):
        first, second = message[0].astype(F32) * ok, message[1].astype(F32)
        for f in range(2):
            tile = first[8 * f:8 * f + 8]
            field[f, near[0], zs, :] = tile
            field[f, near[1], zs, :] = pltpu.roll(tile, 4, 0)
        tile = second[0:8] * ok
        field[0, near[2], zs, :] = tile
        field[1, near[2], zs, :] = pltpu.roll(tile, 4, 0)
        return second[8:16]

    for n, (dx, dz) in enumerate(AROUND):
        halos[n].wait_recv()
        ok = inside(-dx, -dz)
        if dz == 0:
            for f in range(2):
                x0e[f, land_x(dx, 4), OWN_Z, :] = rx[n, pl.ds(4 * f, 4)].astype(F32) * ok
            ce[land_x(dx, 3), OWN_Z, :] = rx[n, pl.ds(8, 3)].astype(F32)
        elif dx == 0:
            unpack_face(rz.at[n - 2], x0e, land_z(dz), ok)
            for m in range(2):
                slab = rz[n - 2, 4 + m].astype(F32)
                for k in range(2):
                    tile = slab[8 * k:8 * k + 8]
                    ce[HX + 4 * m + 2 * k, land_z(dz), :] = tile
                    ce[HX + 4 * m + 2 * k + 1, land_z(dz), :] = pltpu.roll(tile, 4, 0)
        else:
            near = [layer_at(dx, k, True) for k in (1, 2, 3)]
            second = unpack_corner(rc.at[n - 4], x0e, near, land_z(dz), ok)
            ce[near[0], land_z(dz), :] = second
            ce[near[1], land_z(dz), :] = pltpu.roll(second, 4, 0)

    lane_row = iota((1, 128), 1)

    def around(ref, f, x):
        c = ref[f, x]
        total = ref[f, x - 1] + ref[f, x + 1]
        total = total + pltpu.roll(c, 1, 0) + pltpu.roll(c, EZ - 1, 0)
        up, down = pltpu.roll(c, 1, 1), pltpu.roll(c, NY - 1, 1)
        low = jnp.where(lane_row == 0, 0.0, up[:, 0:128]) + down[:, 0:128]
        high = up[:, 128:] + jnp.where(lane_row == 127, 0.0, down[:, 128:])
        return c, total + jnp.concatenate([low, high], axis=1)

    def fold(first, second):
        p = first[HZ:HZ + CZ] * second[HZ:HZ + CZ]
        return (p[0:8, 0:128] + p[8:16, 0:128]) + (p[0:8, 128:256] + p[8:16, 128:256])

    def residual_layer(x):
        made = []
        for f in range(2):
            c, total = around(x0e, f, x)
            diag = 6.0 + LAPLACE_SHIFTS[f] * ce[x]
            r = (srce[f, x] - (diag * c - total)) * mask[x]
            v0[f, x] = r
            made.append((r, r))
        return made

    def apply_layer(src, dst):
        def run(x):
            made = []
            for f in range(2):
                c, total = around(src, f, x)
                diag = (6.0 - CENTRE[f]) + LAPLACE_SHIFTS[f] * ce[x]
                new = (diag * c - total) * mask[x]
                if dst is not None:
                    dst[f, x] = new
                made.append((c, new))
            return made
        return run

    def sweep(layer, width, want):
        def outer(t, _):
            layer(HX - 1 - t)
            layer(HX + CX + t)
            return 0

        def summed(t, carry):
            for x in (HX + 2 * t, HX + 2 * t + 1):
                sums = []
                for c, new in layer(x):
                    for which in want:
                        sums.append(fold(c, new) if which == "cross" else fold(new, new))
                carry = tuple(s + t for s, t in zip(carry, sums))
            return carry

        zero = tuple(jnp.zeros((8, 128), F32) for _ in range(2 * len(want)))
        out = lax.fori_loop(0, CX // 2, summed, zero)
        if width:
            lax.fori_loop(0, width, outer, 0)
        half = len(want)
        return [(out[i], out[half + i]) for i in range(half)]

    def krylov(widths):
        sums = sweep(apply_layer(v0, v1), widths[0], ("cross", "square"))
        sums += sweep(apply_layer(v1, v2), widths[1], ("cross", "square"))
        sums += sweep(apply_layer(v2, None), 0, ("cross",))
        return sums

    low_lanes = iota((8, 128), 1) < 64
    sub = iota((8, 128), 0)

    def start_sum(stage, value):
        asum[stage] = value
        axis = stage % 2

        def push(o, _):
            pltpu.make_async_remote_copy(
                src_ref=asum.at[stage], dst_ref=rsum.at[stage, o - 1],
                send_sem=sum_sem.at[stage, 0], recv_sem=sum_sem.at[stage, 1],
                device_id=at(0, o) if axis == 0 else at(o, 0), device_id_type=MESH).start()
            return 0

        lax.fori_loop(1, NB, push, 0)

    def end_sum(stage):
        everything = pltpu.make_async_remote_copy(
            src_ref=rsum.at[stage], dst_ref=rsum.at[stage],
            send_sem=sum_sem.at[stage, 0], recv_sem=sum_sem.at[stage, 1],
            device_id=at(0, 1), device_id_type=MESH)
        everything.wait_recv()
        return asum[stage] + jnp.sum(rsum[stage], axis=0)

    def pack_sums(sums):
        tile = jnp.zeros((8, 128), F32)
        for k, (s0, s1) in enumerate(sums):
            both = jnp.where(low_lanes, s0 + pltpu.roll(s0, 64, 1), s1 + pltpu.roll(s1, 64, 1))
            tile = jnp.where(sub == k, jnp.sum(both, axis=0, keepdims=True), tile)
        return tile

    def coefficients(tile):
        found = []
        for f in range(2):
            keep = low_lanes if f == 0 else jnp.logical_not(low_lanes)
            column = jnp.sum(jnp.where(keep, tile, 0.0), axis=1, keepdims=True)
            nu = [column[k:k + 1, :] for k in range(2 * ITERS)]
            found.append(cg_coefficients(nu, CENTRE[f]))
        return found

    sums = sweep(residual_layer, 3, ("square",))
    sums += krylov((2, 1))
    start_sum(0, pack_sums(sums))

    def share_cols(o, _):
        pltpu.make_async_remote_copy(
            src_ref=aux.at[pl.ds(16, 16)], dst_ref=cols.at[o - 1], send_sem=cols_sem.at[0], recv_sem=cols_sem.at[1],
            device_id=at(0, o), device_id_type=MESH).start()
        return 0

    lax.fori_loop(1, NB, share_cols, 0)

    own_points = where_points(own_table, 4, 0, 0, 0)
    place_own_receivers()
    here = jnp.where(own_points[0], 1.0, 0.0)
    fields = []
    for ref in (x0e, v0, v1, v2):
        for f in range(2):
            fields.append(ref[f, OWN_X, OWN_Z, :].reshape(ROWS, NY))
    fields = jnp.concatenate(fields, axis=0)
    head = fields.astype(BF16)
    tail = (fields - head.astype(F32)).astype(BF16)
    columns = lax.dot_general(head, own_points[1], (((1,), (0,)), ((), ())), preferred_element_type=F32)
    columns += lax.dot_general(tail, own_points[1], (((1,), (0,)), ((), ())), preferred_element_type=F32)
    for j in range(8):
        row = jnp.sum(columns[ROWS * j:ROWS * (j + 1)] * here, axis=0, keepdims=True)
        seen[j:j + 1, :] = row - own_table[7 + j:8 + j, :] if j < 2 else row
    for n, (dx, dz) in enumerate(AROUND):
        pltpu.make_async_remote_copy(
            src_ref=seen, dst_ref=rseen.at[n], send_sem=seen_sem.at[0], recv_sem=seen_sem.at[1],
            device_id=at(dx, dz), device_id_type=MESH).start()
    point_values = pltpu.make_async_remote_copy(
        src_ref=rseen, dst_ref=rseen, send_sem=seen_sem.at[0], recv_sem=seen_sem.at[1],
        device_id=at(1, 0), device_id_type=MESH)
    around_points = []
    for n, (dx, dz) in enumerate(AROUND):
        hit, along_y, xs, zs, shape = where_points(rlist[n], 4, -dx, -dz, 3)
        rec_y[n] = along_y
        count = shape[0] * shape[1]
        rec_hit[n, pl.ds(0, count)] = jnp.where(hit, 1.0, 0.0)
        around_points.append((xs, zs, shape, count))
    for n, (dx, dz) in enumerate(AROUND):
        adjoint_halos[n].wait_recv()
        ok = inside(-dx, -dz)
        if dz == 0:
            for f in range(2):
                a0e[f, land_x(dx, 4), OWN_Z, :] = bx[n, pl.ds(4 * f, 4)].astype(F32) * ok
        elif dx == 0:
            unpack_face(bz.at[n - 2], a0e, land_z(dz), ok)
        else:
            unpack_corner(bc.at[n - 4], a0e, [layer_at(dx, k, True) for k in (1, 2, 3)], land_z(dz), ok)

    start_sum(1, end_sum(0))

    def adjoint_part(t, _):
        for x in (HX - 3 + 2 * t, HX - 2 + 2 * t):
            for f in range(2):
                c, total = around(a0e, f, x)
                diag = 6.0 + LAPLACE_SHIFTS[f] * ce[x]
                w[f, x] = (diag * c - total) * mask[x]
        return 0

    lax.fori_loop(0, CX // 2 + 3, adjoint_part, 0)

    pltpu.make_async_remote_copy(
        src_ref=cols.at[pl.ds(0, NB - 1)], dst_ref=cols.at[pl.ds(0, NB - 1)],
        send_sem=cols_sem.at[0], recv_sem=cols_sem.at[1],
        device_id=at(0, 1), device_id_type=MESH).wait_recv()
    cols[NB - 1] = aux[16:32, :]
    first_row = (d * ROWS).astype(F32)
    row_lane = iota((NNZ, 128), 1).astype(F32)

    def request(slot, _):
        row = 2.0 * cols[slot] - first_row
        hot = jnp.concatenate([jnp.where(row == row_lane, 1.0, 0.0), jnp.where(row + 1.0 == row_lane, 1.0, 0.0)], axis=0)
        pick_hot[pl.ds(pl.multiple_of(slot * 2 * NNZ, 2 * NNZ), 2 * NNZ)] = hot.astype(BF16)
        return 0

    lax.fori_loop(0, NB, request, 0)

    point_values.wait_recv()
    found = coefficients(end_sum(1))

    for n, (dx, dz) in enumerate(AROUND):
        xs, zs, shape, count = around_points[n]
        ok = inside(-dx, -dz)
        left = []
        for f in range(2):
            a = found[f]
            values = rseen[n, f:f + 1, :]
            for k in range(ITERS):
                values = values + a[k] * rseen[n, 2 * (k + 1) + f:2 * (k + 1) + f + 1, :]
            left.append((rec_hit[n, pl.ds(0, count)] * parts(values, ok)).astype(BF16))
        placed = lax.dot_general(jnp.concatenate(left, axis=0), rec_y[n], (((1,), (1,)), ((), ())),
                                 preferred_element_type=F32).reshape((2,) + shape + (NY,))
        v0[:, xs, zs, :] = placed - w[:, xs, zs, :]

    def own_residual(t, carry):
        for x in (HX + 2 * t, HX + 2 * t + 1):
            out = []
            for f in range(2):
                a = found[f]
                new = x0e[f, x, OWN_Z, :] + a[0] * v0[f, x, OWN_Z, :] + a[1] * v1[f, x, OWN_Z, :]
                new = new + a[2] * v2[f, x, OWN_Z, :]
                fwd[f, x - HX] = new
                u = cnte[x - HX] * new - obse[f, x - HX] - w[f, x, OWN_Z, :]
                v0[f, x, OWN_Z, :] = u
                p = u * u
                out.append(carry[f] + (p[0:8, 0:128] + p[8:16, 0:128]) + (p[0:8, 128:256] + p[8:16, 128:256]))
            carry = tuple(out)
        return carry

    squares = lax.fori_loop(0, CX // 2, own_residual, (jnp.zeros((8, 128), F32),) * 2)
    forward_store = pltpu.make_async_copy(fwd, fwd_out, out_sem.at[0])
    forward_store.start()

    sums = [squares] + krylov((2, 1))
    start_sum(2, pack_sums(sums))
    start_sum(3, end_sum(2))
    found_adjoint = coefficients(end_sum(3))

    def gradient_layer(x, _):
        total = jnp.zeros((CZ, NY), F32)
        for f in range(2):
            e = found_adjoint[f]
            own = a0e[f, x + HX, OWN_Z, :] + e[0] * v0[f, x + HX, OWN_Z, :] + e[1] * v1[f, x + HX, OWN_Z, :]
            own = own + e[2] * v2[f, x + HX, OWN_Z, :]
            total = total + LAPLACE_SHIFTS[f] * fwd[f, x] * own
        grad[pl.ds(pl.multiple_of(x * CZ, CZ), CZ)] = (-total).astype(BF16)
        return 0

    lax.fori_loop(0, CX, gradient_layer, 0)

    psend[...] = jnp.dot(pick_hot[...], grad[...], preferred_element_type=F32).astype(BF16).reshape(NB, 2 * NNZ, NY)

    def answer(o, _):
        pltpu.make_async_remote_copy(
            src_ref=psend.at[NB - 1 - o], dst_ref=precv.at[o - 1], send_sem=pick_sem.at[0], recv_sem=pick_sem.at[1],
            device_id=at(0, o), device_id_type=MESH).start()
        return 0

    lax.fori_loop(1, NB, answer, 0)
    cov_load.wait()
    picks = pltpu.make_async_remote_copy(
        src_ref=precv, dst_ref=precv, send_sem=pick_sem.at[0], recv_sem=pick_sem.at[1],
        device_id=at(0, 1), device_id_type=MESH)
    picks.wait_recv()
    picked = psend[NB - 1].astype(F32) + jnp.sum(precv[...].astype(F32), axis=0)
    picked = picked.astype(BF16)

    term_row = iota((NNZ, BLOCK), 0)

    def term(t, total):
        for k in (4 * t, 4 * t + 1, 4 * t + 2, 4 * t + 3):
            block = cov[k]
            made = lax.dot_general(picked[0:NNZ], block[:, 0:NY], (((1,), (1,)), ((), ())), preferred_element_type=F32)
            made += lax.dot_general(picked[NNZ:], block[:, NY:], (((1,), (1,)), ((), ())), preferred_element_type=F32)
            total = jnp.where(term_row == k, made, total)
        return total

    terms = lax.fori_loop(0, NNZ // 4, term, jnp.zeros((NNZ, BLOCK), F32))
    cov_rows = rows_v[0].astype(F32)
    out_row = iota((ROWS, NNZ), 0).astype(F32)
    total = grad[...].astype(F32)
    for half in range(2):
        hot = jnp.where(2.0 * cov_rows + float(half) == out_row, 1.0, 0.0)
        total = total + jnp.dot(hot, terms[:, half * NY:(half + 1) * NY], precision=lax.Precision.HIGHEST,
                                preferred_element_type=F32)
    pre[...] = total.reshape(CX, CZ, NY)
    pre_store = pltpu.make_async_copy(pre, pre_out, out_sem.at[1])
    pre_store.start()

    lists.wait_send()
    for copy in halos + adjoint_halos + [point_values]:
        copy.wait_send()
    pltpu.make_async_remote_copy(
        src_ref=cols.at[pl.ds(0, NB - 1)], dst_ref=cols.at[pl.ds(0, NB - 1)],
        send_sem=cols_sem.at[0], recv_sem=cols_sem.at[1],
        device_id=at(0, 1), device_id_type=MESH).wait_send()
    for stage in range(4):
        pltpu.make_async_remote_copy(
            src_ref=rsum.at[stage], dst_ref=rsum.at[stage],
            send_sem=sum_sem.at[stage, 0], recv_sem=sum_sem.at[stage, 1],
            device_id=at(0, 1), device_id_type=MESH).wait_send()
    picks.wait_send()
    forward_store.wait()
    pre_store.wait()


def hand_over(fwd_in, pre_in, fwd_out, pre_out):
    fwd_out[...] = fwd_in[...]
    pre_out[...] = pre_in[...]


def local(conductivity, initial_field, adjoint_initial, src_cell, src_amp, rec_cell, observed, cov_blocks, cov_rows, cov_cols):
    big = pltpu.VMEM((2, EX, EZ, NY), F32)
    one = pltpu.VMEM((EX, EZ, NY), F32)
    dma = pltpu.SemaphoreType.DMA
    scratch = [
        pltpu.VMEM(src_cell.shape, jnp.int32), pltpu.VMEM(src_amp.shape, F32),
        pltpu.VMEM(rec_cell.shape, jnp.int32), pltpu.VMEM(observed.shape, F32),
        pltpu.VMEM(cov_rows.shape, jnp.int32), pltpu.VMEM(cov_cols.shape, jnp.int32),
        pltpu.VMEM((32, 128), F32), pltpu.VMEM((NNZ, BLOCK, BLOCK), BF16),
        one, big, big, one, big,
        pltpu.VMEM((2, CX, CZ, NY), F32), pltpu.VMEM((CX, CZ, NY), F32),
        big, big, big, big,
        pltpu.VMEM((2, CX, CZ, NY), F32), pltpu.VMEM((ROWS, NY), BF16), pltpu.VMEM((CX, CZ, NY), F32),
        pltpu.VMEM((2 * NNZ * NB, ROWS), BF16),
    ]
    for count, slabs in ((2, 11), (2, 6), (4, 2), (2, 8), (2, 4), (4, 2)):
        scratch += [pltpu.VMEM((count, slabs, 16, NY), BF16)] * 2
    scratch += [
        pltpu.VMEM((8, 16, 128), F32), pltpu.VMEM((8, 128), F32), pltpu.VMEM((8, 8, 128), F32),
        pltpu.VMEM((8, 64, 128), F32), pltpu.VMEM((8, NY, 128), BF16), pltpu.VMEM((NB, NNZ, 128), F32),
        pltpu.VMEM((4, 8, 128), F32), pltpu.VMEM((4, NB - 1, 8, 128), F32),
        pltpu.VMEM((NB, 2 * NNZ, NY), BF16), pltpu.VMEM((NB - 1, 2 * NNZ, NY), BF16),
        dma((9,)), dma, dma((2,)), dma((2,)), dma((2,)), dma((8, 2)), dma((8, 2)), dma((2,)), dma((4, 2)), dma((2,)),
    ]
    anywhere = pl.BlockSpec(memory_space=pl.ANY)
    results = pl.pallas_call(
        kernel,
        out_shape=(
            jax.ShapeDtypeStruct((2, CX, CZ, NY), F32),
            jax.ShapeDtypeStruct((CX, CZ, NY), F32),
        ),
        in_specs=[anywhere] * 10,
        out_specs=(anywhere, anywhere),
        scratch_shapes=scratch,
        compiler_params=pltpu.CompilerParams(
            collective_id=0, has_side_effects=True, vmem_limit_bytes=56 * 2**20),
    )(conductivity, initial_field, adjoint_initial, src_cell, src_amp, rec_cell, observed,
      cov_blocks.reshape(NNZ, BLOCK, BLOCK), cov_rows, cov_cols)
    return pl.pallas_call(
        hand_over,
        out_shape=[jax.ShapeDtypeStruct(r.shape, r.dtype) for r in results],
    )(*results)


def solution(mesh):
    return jax.shard_map(
        local,
        mesh=mesh,
        in_specs=(
            P("brick", "depth", None),
            P(None, "brick", "depth", None),
            P(None, "brick", "depth", None),
            P("brick", "depth", None),
            P("brick", "depth", None, None),
            P("brick", "depth", None),
            P("brick", "depth", None, None),
            P("brick", "depth", None, None, None),
            P("brick", "depth", None),
            P("brick", "depth", None),
        ),
        out_specs=(P(None, "brick", "depth", None), P("brick", "depth", None)),
        check_vma=False,
    )
```

```python
import functools

import jax
import jax.numpy as jnp
from jax import lax
from jax.experimental import pallas as pl
from jax.experimental.pallas import tpu as pltpu
from jax.sharding import PartitionSpec as P

LAPLACE_SHIFTS = (0.5, 2.0)
CENTRE = (6.5, 8.0)
ITERS = 3
NB = 16
CX, CZ, NY = 8, 16, 256
HX, HZ = 6, 8
EX, EZ = CX + 2 * HX, CZ + 2 * HZ
NNZ, BLOCK = 16, 512
ROWS = CX * CZ
F32, BF16 = jnp.float32, jnp.bfloat16
MESH = pl.DeviceIdType.MESH
OWN_X, OWN_Z = pl.ds(HX, CX), pl.ds(HZ, CZ)

FACES_X = ((1, 0), (-1, 0))
FACES_Z = ((0, 1), (0, -1))
CORNERS = ((1, 1), (1, -1), (-1, 1), (-1, -1))
AROUND = FACES_X + FACES_Z + CORNERS

STEPS = sorted(
    ((i, j, k, c) for i in range(4) for j in range(4) for k in range(8) for c in range(2)),
    key=lambda s: -(8 * (min(s[0], 4 - s[0]) + min(s[1], 4 - s[1]) + min(s[2], 8 - s[2])) + s[3]))
PLANE = [s for s in STEPS if s[2:] == (0, 0) and s[:2] != (0, 0)]
COLUMN = [s for s in STEPS if s[:2] == (0, 0) and s[2:] != (0, 0)]
LAYERS = [s for s in STEPS if s[2] == 0 and s[1] % 2 == 0 and s != (0, 0, 0, 0)]


def iota(shape, dim):
    return lax.broadcasted_iota(jnp.int32, shape, dim)


def send_x(dx, width, skip=0):
    return pl.ds(HX + CX - skip - width, width) if dx > 0 else pl.ds(HX + skip, width)


def send_z(dz):
    return pl.ds(HZ + CZ - HZ, HZ) if dz > 0 else pl.ds(HZ, HZ)


def land_x(dx, width, skip=0):
    return pl.ds(HX - skip - width, width) if dx > 0 else pl.ds(HX + CX + skip, width)


def land_z(dz):
    return pl.ds(0, HZ) if dz > 0 else pl.ds(HZ + CZ, HZ)


def layer_at(dx, distance, land):
    if land:
        return HX - distance if dx > 0 else HX + CX + distance - 1
    return HX + CX - distance if dx > 0 else HX + distance - 1


def halves(first, second, dz):
    near = (iota((8, 1), 0) >= 4) if dz > 0 else (iota((8, 1), 0) < 4)
    return jnp.where(near, first, pltpu.roll(second, 4, 0))


def pack_face(field, dz):
    slabs = []
    for m in range(CX // 2):
        tiles = [halves(field[f][2 * m], field[f][2 * m + 1], dz) for f in range(2)]
        slabs.append(jnp.concatenate(tiles, axis=0).astype(BF16))
    return slabs


def pack_corner(field, near, zs, dz):
    tiles = [halves(field[f, near[0], zs, :], field[f, near[1], zs, :], dz) for f in range(2)]
    return tiles + [halves(field[0, near[2], zs, :], field[1, near[2], zs, :], dz)]


def cg_coefficients(nu, centre):
    def inner(p, q, shift):
        total = None
        for i, pi in enumerate(p):
            for j, qj in enumerate(q):
                term = pi * qj * nu[i + j + shift]
                total = term if total is None else total + term
        return total

    one = jnp.ones_like(nu[0])
    r, p = [one], [one]
    rr = nu[0]
    x = [jnp.zeros_like(one)] * ITERS
    for it in range(ITERS):
        step = rr / (inner(p, p, 1) + centre * inner(p, p, 0))
        for i, pi in enumerate(p):
            x[i] = x[i] + step * pi
        if it + 1 < ITERS:
            ap = [centre * pi for pi in p] + [jnp.zeros_like(one)]
            for i, pi in enumerate(p):
                ap[i + 1] = ap[i + 1] + pi
            r = r + [jnp.zeros_like(one)]
            r = [ri - step * ai for ri, ai in zip(r, ap)]
            new = inner(r, r, 0)
            beta = new / rr
            p = p + [jnp.zeros_like(one)]
            p = [ri + beta * pi for ri, pi in zip(r, p)]
            rr = new
    return x


def kernel(
    cond_in, x0_in, a0_in, src_in, amp_in, rec_in, obs_in, cov_in, rows_in, cols_in,
    fwd_out, pre_out,
    src_v, amp_v, rec_v, obs_v, rows_v, cols_v, aux, cov, ce, x0e, a0e, mask, srce, obse, cnte, v0, v1, v2, w, fwd, grad, pre, pick_hot,
    sx, rx, sz, rz, sc, rc, ax, bx, az, bz, ac, bc,
    rlist, seen, rseen, rec_hit, rec_y, cols, asum, rsum, psend, precv,
    in_sem, cov_sem, out_sem, list_sem, cols_sem, halo_sem, adj_sem, seen_sem, sum_sem, pick_sem,
):
    b, d = lax.axis_index("brick"), lax.axis_index("depth")

    def at(dx, dz):
        return lax.rem(b + dx + NB, NB), lax.rem(d + dz + NB, NB)

    barrier = pltpu.get_barrier_semaphore()
    for dx, dz in FACES_X + CORNERS:
        pl.semaphore_signal(barrier, inc=1, device_id=at(dx, dz), device_id_type=MESH)

    cx, cy = lax.div(d, 4), 2 * lax.rem(lax.div(d, 2), 2) + lax.div(b, 8)
    cz, core = lax.rem(b, 8), lax.rem(d, 2)

    def beside(step):
        x, y = lax.rem(cx + step[0], 4), lax.rem(cy + step[1], 4)
        return lax.rem(y, 2) * 8 + lax.rem(cz + step[2], 8), x * 4 + lax.div(y, 2) * 2 + lax.rem(core + step[3], 2)

    greeted = LAYERS + [s for s in PLANE if s[1] % 2] + [s for s in COLUMN if s[2]]
    for step in greeted:
        pl.semaphore_signal(barrier, inc=1, device_id=beside(step), device_id_type=MESH)

    loads = [
        pltpu.make_async_copy(x0_in, x0e.at[:, OWN_X, OWN_Z, :], in_sem.at[0]),
        pltpu.make_async_copy(cond_in, ce.at[OWN_X, OWN_Z, :], in_sem.at[1]),
        pltpu.make_async_copy(src_in, src_v, in_sem.at[2]),
        pltpu.make_async_copy(amp_in, amp_v, in_sem.at[3]),
        pltpu.make_async_copy(rec_in, rec_v, in_sem.at[4]),
        pltpu.make_async_copy(obs_in, obs_v, in_sem.at[5]),
        pltpu.make_async_copy(rows_in, rows_v, in_sem.at[6]),
        pltpu.make_async_copy(cols_in, cols_v, in_sem.at[7]),
        pltpu.make_async_copy(a0_in, a0e.at[:, OWN_X, OWN_Z, :], in_sem.at[8]),
    ]
    for load in loads:
        load.start()
    cov_load = pltpu.make_async_copy(cov_in, cov, cov_sem)
    cov_load.start()

    for load in loads[:2]:
        load.wait()
    for i, (dx, _) in enumerate(FACES_X):
        for f in range(2):
            sx[i, pl.ds(4 * f, 4)] = x0e[f, send_x(dx, 4), OWN_Z, :].astype(BF16)
        sx[i, pl.ds(8, 3)] = ce[send_x(dx, 3), OWN_Z, :].astype(BF16)
    for i, (_, dz) in enumerate(FACES_Z):
        zs = send_z(dz)
        for m, slab in enumerate(pack_face([x0e[f, OWN_X, zs, :] for f in range(2)], dz)):
            sz[i, m] = slab
        for m in range(2):
            tiles = [halves(ce[HX + k, zs, :], ce[HX + k + 1, zs, :], dz) for k in (4 * m, 4 * m + 2)]
            sz[i, 4 + m] = jnp.concatenate(tiles, axis=0).astype(BF16)
    for i, (dx, dz) in enumerate(CORNERS):
        zs = send_z(dz)
        near = [layer_at(dx, k, False) for k in (1, 2, 3)]
        tiles = pack_corner(x0e, near, zs, dz)
        tiles.append(halves(ce[near[0], zs, :], ce[near[1], zs, :], dz))
        sc[i, 0] = jnp.concatenate(tiles[:2], axis=0).astype(BF16)
        sc[i, 1] = jnp.concatenate(tiles[2:], axis=0).astype(BF16)

    for load in loads[2:8]:
        load.wait()

    def twice(row):
        return jnp.concatenate([row, row], axis=1)

    src_cell, rec_cell = src_v[0], rec_v[0]
    aux[0:1, :] = twice((src_cell >> 8).astype(F32))
    aux[1:2, :] = twice((src_cell & (NY - 1)).astype(F32))
    aux[2:4, :] = twice(amp_v[0, 0])
    aux[4:5, :] = twice((rec_cell >> 8).astype(F32))
    aux[5:6, :] = twice((rec_cell & (NY - 1)).astype(F32))
    aux[6:7, :] = jnp.where(iota((1, 128), 1) < 64, 1.0, 0.0)
    aux[7:9, :] = twice(obs_v[0, 0])
    aux[9:16, :] = jnp.zeros((7, 128), F32)
    col_row = jnp.where(iota((NNZ, NNZ), 0) == iota((NNZ, NNZ), 1), cols_v[0].astype(F32), 0.0)
    aux[16:32, :] = jnp.broadcast_to(jnp.sum(col_row, axis=1, keepdims=True), (NNZ, 128))

    pl.semaphore_wait(barrier, len(FACES_X) + len(CORNERS) + len(greeted))

    for n, (dx, dz) in enumerate(AROUND):
        pltpu.make_async_remote_copy(
            src_ref=aux.at[pl.ds(0, 16)], dst_ref=rlist.at[n], send_sem=list_sem.at[0], recv_sem=list_sem.at[1],
            device_id=at(dx, dz), device_id_type=MESH).start()

    def exchange(n, dx, dz, src, dst, sems):
        return pltpu.make_async_remote_copy(
            src_ref=src, dst_ref=dst, send_sem=sems.at[n, 0], recv_sem=sems.at[n, 1],
            device_id=at(dx, dz), device_id_type=MESH)

    halos = []
    for group, s, r in ((FACES_X, sx, rx), (FACES_Z, sz, rz), (CORNERS, sc, rc)):
        for i, (dx, dz) in enumerate(group):
            halos.append(exchange(len(halos), dx, dz, s.at[i], r.at[i], halo_sem))
    for copy in reversed(halos):
        copy.start()

    def inside(dx, dz):
        bx_, dz_ = b + dx, d + dz
        ok = (bx_ >= 0) & (bx_ < NB) & (dz_ >= 0) & (dz_ < NB)
        return jnp.where(ok, 1.0, 0.0).astype(F32)

    for i, (dx, dz) in enumerate(((0, 0),) + AROUND):
        xs = pl.ds(HX, CX) if dx == 0 else land_x(-dx, HX)
        zs = pl.ds(HZ, CZ) if dz == 0 else land_z(-dz)
        nx, nz = (CX if dx == 0 else HX), (CZ if dz == 0 else HZ)
        mask[xs, zs, :] = jnp.full((nx, nz, NY), inside(dx, dz), F32)

    for zs in (pl.ds(0, HZ), pl.ds(HZ + CZ, HZ)):
        for xs in (pl.ds(0, 3), pl.ds(EX - 3, 3)):
            x0e[:, xs, zs, :] = jnp.zeros((2, 3, HZ, NY), F32)
            a0e[:, xs, zs, :] = jnp.zeros((2, 3, HZ, NY), F32)
        for xs in (pl.ds(0, 4), pl.ds(EX - 4, 4)):
            ce[xs, zs, :] = jnp.zeros((4, HZ, NY), F32)

    lane = iota((1, 128), 1)

    def parts(row, ok):
        value = row * ok
        head = value.astype(BF16).astype(F32)
        return jnp.where(lane < 64, head, value - head)

    def where_points(table, base, dx, dz, width):
        xs = pl.ds(HX, CX) if dx == 0 else land_x(-dx, width)
        zs = pl.ds(HZ, CZ) if dz == 0 else land_z(-dz)
        nx, x_low = (CX, 0) if dx == 0 else ((width, 0) if dx > 0 else (width, CX - width))
        nz, z_low = (CZ, 0) if dz == 0 else ((HZ, 0) if dz > 0 else (HZ, CZ - HZ))
        shape = (nx, nz, 128)
        cell_row = ((iota(shape, 0) + x_low) * CZ + iota(shape, 1) + z_low).reshape(nx * nz, 128).astype(F32)
        hit = cell_row == table[base:base + 1, :]
        along_y = (iota((NY, 128), 0).astype(F32) == table[base + 1:base + 2, :]).astype(F32).astype(BF16)
        return hit, along_y, xs, zs, (nx, nz)

    def place(hit, along_y, rows, shape):
        left = jnp.concatenate([jnp.where(hit, row, 0.0).astype(BF16) for row in rows], axis=0)
        placed = lax.dot_general(left, along_y, (((1,), (1,)), ((), ())), preferred_element_type=F32)
        return placed.reshape((len(rows),) + shape + (NY,))

    def place_sources(table, dx, dz):
        ok = inside(dx, dz)
        hit, along_y, xs, zs, shape = where_points(table, 0, dx, dz, 3)
        srce[:, xs, zs, :] = place(hit, along_y, [parts(table[2 + f:3 + f, :], ok) for f in range(2)], shape)

    def place_own_receivers():
        rows = [own_table[6:7, :]] + [parts(own_table[7 + f:8 + f, :], 1.0) for f in range(2)]
        placed = place(*own_points[:2], rows, own_points[4])
        cnte[...] = placed[0]
        obse[...] = placed[1:3]

    own_table = aux[0:16, :]
    place_sources(own_table, 0, 0)

    loads[8].wait()
    for i, (dx, _) in enumerate(FACES_X):
        for f in range(2):
            ax[i, pl.ds(4 * f, 4)] = a0e[f, send_x(dx, 4), OWN_Z, :].astype(BF16)
    for i, (_, dz) in enumerate(FACES_Z):
        for m, slab in enumerate(pack_face([a0e[f, OWN_X, send_z(dz), :] for f in range(2)], dz)):
            az[i, m] = slab
    for i, (dx, dz) in enumerate(CORNERS):
        tiles = pack_corner(a0e, [layer_at(dx, k, False) for k in (1, 2, 3)], send_z(dz), dz)
        ac[i, 0] = jnp.concatenate(tiles[:2], axis=0).astype(BF16)
        ac[i, 1] = jnp.concatenate([tiles[2], tiles[2]], axis=0).astype(BF16)
    adjoint_halos = []
    for group, s, r in ((FACES_X, ax, bx), (FACES_Z, az, bz), (CORNERS, ac, bc)):
        for i, (dx, dz) in enumerate(group):
            adjoint_halos.append(exchange(len(adjoint_halos), dx, dz, s.at[i], r.at[i], adj_sem))

    lists = pltpu.make_async_remote_copy(
        src_ref=rlist, dst_ref=rlist, send_sem=list_sem.at[0], recv_sem=list_sem.at[1],
        device_id=at(1, 0), device_id_type=MESH)
    lists.wait_recv()
    for n, (dx, dz) in enumerate(AROUND):
        place_sources(rlist[n], -dx, -dz)
    for copy in adjoint_halos:
        copy.start()

    def unpack_face(message, field, zs, ok):
        for m in range(CX // 2):
            slab = message[m].astype(F32) * ok
            for f in range(2):
                tile = slab[8 * f:8 * f + 8]
                field[f, HX + 2 * m, zs, :] = tile
                field[f, HX + 2 * m + 1, zs, :] = pltpu.roll(tile, 4, 0)

    def unpack_corner(message, field, near, zs, ok):
        first, second = message[0].astype(F32) * ok, message[1].astype(F32)
        for f in range(2):
            tile = first[8 * f:8 * f + 8]
            field[f, near[0], zs, :] = tile
            field[f, near[1], zs, :] = pltpu.roll(tile, 4, 0)
        tile = second[0:8] * ok
        field[0, near[2], zs, :] = tile
        field[1, near[2], zs, :] = pltpu.roll(tile, 4, 0)
        return second[8:16]

    for n, (dx, dz) in enumerate(AROUND):
        halos[n].wait_recv()
        ok = inside(-dx, -dz)
        if dz == 0:
            for f in range(2):
                x0e[f, land_x(dx, 4), OWN_Z, :] = rx[n, pl.ds(4 * f, 4)].astype(F32) * ok
            ce[land_x(dx, 3), OWN_Z, :] = rx[n, pl.ds(8, 3)].astype(F32)
        elif dx == 0:
            unpack_face(rz.at[n - 2], x0e, land_z(dz), ok)
            for m in range(2):
                slab = rz[n - 2, 4 + m].astype(F32)
                for k in range(2):
                    tile = slab[8 * k:8 * k + 8]
                    ce[HX + 4 * m + 2 * k, land_z(dz), :] = tile
                    ce[HX + 4 * m + 2 * k + 1, land_z(dz), :] = pltpu.roll(tile, 4, 0)
        else:
            near = [layer_at(dx, k, True) for k in (1, 2, 3)]
            second = unpack_corner(rc.at[n - 4], x0e, near, land_z(dz), ok)
            ce[near[0], land_z(dz), :] = second
            ce[near[1], land_z(dz), :] = pltpu.roll(second, 4, 0)

    lane_row = iota((1, 128), 1)

    def around(ref, f, x):
        c = ref[f, x]
        total = ref[f, x - 1] + ref[f, x + 1]
        total = total + pltpu.roll(c, 1, 0) + pltpu.roll(c, EZ - 1, 0)
        up, down = pltpu.roll(c, 1, 1), pltpu.roll(c, NY - 1, 1)
        low = jnp.where(lane_row == 0, 0.0, up[:, 0:128]) + down[:, 0:128]
        high = up[:, 128:] + jnp.where(lane_row == 127, 0.0, down[:, 128:])
        return c, total + jnp.concatenate([low, high], axis=1)

    def fold(first, second):
        p = first[HZ:HZ + CZ] * second[HZ:HZ + CZ]
        return (p[0:8, 0:128] + p[8:16, 0:128]) + (p[0:8, 128:256] + p[8:16, 128:256])

    def residual_layer(x):
        made = []
        for f in range(2):
            c, total = around(x0e, f, x)
            diag = 6.0 + LAPLACE_SHIFTS[f] * ce[x]
            r = (srce[f, x] - (diag * c - total)) * mask[x]
            v0[f, x] = r
            made.append((r, r))
        return made

    def apply_layer(src, dst):
        def run(x):
            made = []
            for f in range(2):
                c, total = around(src, f, x)
                diag = (6.0 - CENTRE[f]) + LAPLACE_SHIFTS[f] * ce[x]
                new = (diag * c - total) * mask[x]
                if dst is not None:
                    dst[f, x] = new
                made.append((c, new))
            return made
        return run

    def sweep(layer, width, want):
        def outer(t, _):
            layer(HX - 1 - t)
            layer(HX + CX + t)
            return 0

        def summed(t, carry):
            for x in (HX + 2 * t, HX + 2 * t + 1):
                sums = []
                for c, new in layer(x):
                    for which in want:
                        sums.append(fold(c, new) if which == "cross" else fold(new, new))
                carry = tuple(s + t for s, t in zip(carry, sums))
            return carry

        zero = tuple(jnp.zeros((8, 128), F32) for _ in range(2 * len(want)))
        out = lax.fori_loop(0, CX // 2, summed, zero)
        if width:
            lax.fori_loop(0, width, outer, 0)
        half = len(want)
        return [(out[i], out[half + i]) for i in range(half)]

    def krylov(widths):
        sums = sweep(apply_layer(v0, v1), widths[0], ("cross", "square"))
        sums += sweep(apply_layer(v1, v2), widths[1], ("cross", "square"))
        sums += sweep(apply_layer(v2, None), 0, ("cross",))
        return sums

    low_lanes = iota((8, 128), 1) < 64
    sub = iota((8, 128), 0)

    def start_sum(stage, value):
        asum[stage] = value
        for i, step in enumerate(COLUMN if stage % 2 else PLANE):
            pltpu.make_async_remote_copy(
                src_ref=asum.at[stage], dst_ref=rsum.at[stage, i],
                send_sem=sum_sem.at[stage, 0], recv_sem=sum_sem.at[stage, 1],
                device_id=beside(step), device_id_type=MESH).start()

    def end_sum(stage):
        everything = pltpu.make_async_remote_copy(
            src_ref=rsum.at[stage], dst_ref=rsum.at[stage],
            send_sem=sum_sem.at[stage, 0], recv_sem=sum_sem.at[stage, 1],
            device_id=at(0, 1), device_id_type=MESH)
        everything.wait_recv()
        return asum[stage] + jnp.sum(rsum[stage], axis=0)

    def pack_sums(sums):
        tile = jnp.zeros((8, 128), F32)
        for k, (s0, s1) in enumerate(sums):
            both = jnp.where(low_lanes, s0 + pltpu.roll(s0, 64, 1), s1 + pltpu.roll(s1, 64, 1))
            tile = jnp.where(sub == k, jnp.sum(both, axis=0, keepdims=True), tile)
        return tile

    def coefficients(tile):
        found = []
        for f in range(2):
            keep = low_lanes if f == 0 else jnp.logical_not(low_lanes)
            column = jnp.sum(jnp.where(keep, tile, 0.0), axis=1, keepdims=True)
            nu = [column[k:k + 1, :] for k in range(2 * ITERS)]
            found.append(cg_coefficients(nu, CENTRE[f]))
        return found

    sums = sweep(residual_layer, 3, ("square",))
    sums += krylov((2, 1))
    start_sum(0, pack_sums(sums))

    for i, step in enumerate(LAYERS):
        pltpu.make_async_remote_copy(
            src_ref=aux.at[pl.ds(16, 16)], dst_ref=cols.at[i], send_sem=cols_sem.at[0], recv_sem=cols_sem.at[1],
            device_id=beside(step), device_id_type=MESH).start()

    own_points = where_points(own_table, 4, 0, 0, 0)
    place_own_receivers()
    here = jnp.where(own_points[0], 1.0, 0.0)
    fields = []
    for ref in (x0e, v0, v1, v2):
        for f in range(2):
            fields.append(ref[f, OWN_X, OWN_Z, :].reshape(ROWS, NY))
    fields = jnp.concatenate(fields, axis=0)
    head = fields.astype(BF16)
    tail = (fields - head.astype(F32)).astype(BF16)
    columns = lax.dot_general(head, own_points[1], (((1,), (0,)), ((), ())), preferred_element_type=F32)
    columns += lax.dot_general(tail, own_points[1], (((1,), (0,)), ((), ())), preferred_element_type=F32)
    for j in range(8):
        row = jnp.sum(columns[ROWS * j:ROWS * (j + 1)] * here, axis=0, keepdims=True)
        seen[j:j + 1, :] = row - own_table[7 + j:8 + j, :] if j < 2 else row
    for n, (dx, dz) in enumerate(AROUND):
        pltpu.make_async_remote_copy(
            src_ref=seen, dst_ref=rseen.at[n], send_sem=seen_sem.at[0], recv_sem=seen_sem.at[1],
            device_id=at(dx, dz), device_id_type=MESH).start()
    point_values = pltpu.make_async_remote_copy(
        src_ref=rseen, dst_ref=rseen, send_sem=seen_sem.at[0], recv_sem=seen_sem.at[1],
        device_id=at(1, 0), device_id_type=MESH)
    around_points = []
    for n, (dx, dz) in enumerate(AROUND):
        hit, along_y, xs, zs, shape = where_points(rlist[n], 4, -dx, -dz, 3)
        rec_y[n] = along_y
        count = shape[0] * shape[1]
        rec_hit[n, pl.ds(0, count)] = jnp.where(hit, 1.0, 0.0)
        around_points.append((xs, zs, shape, count))
    for n, (dx, dz) in enumerate(AROUND):
        adjoint_halos[n].wait_recv()
        ok = inside(-dx, -dz)
        if dz == 0:
            for f in range(2):
                a0e[f, land_x(dx, 4), OWN_Z, :] = bx[n, pl.ds(4 * f, 4)].astype(F32) * ok
        elif dx == 0:
            unpack_face(bz.at[n - 2], a0e, land_z(dz), ok)
        else:
            unpack_corner(bc.at[n - 4], a0e, [layer_at(dx, k, True) for k in (1, 2, 3)], land_z(dz), ok)

    start_sum(1, end_sum(0))

    def adjoint_part(t, _):
        for x in (HX - 3 + 2 * t, HX - 2 + 2 * t):
            for f in range(2):
                c, total = around(a0e, f, x)
                diag = 6.0 + LAPLACE_SHIFTS[f] * ce[x]
                w[f, x] = (diag * c - total) * mask[x]
        return 0

    lax.fori_loop(0, CX // 2 + 3, adjoint_part, 0)

    pltpu.make_async_remote_copy(
        src_ref=cols.at[pl.ds(0, NB - 1)], dst_ref=cols.at[pl.ds(0, NB - 1)],
        send_sem=cols_sem.at[0], recv_sem=cols_sem.at[1],
        device_id=at(0, 1), device_id_type=MESH).wait_recv()
    cols[NB - 1] = aux[16:32, :]
    first_row = (d * ROWS).astype(F32)
    row_lane = iota((NNZ, 128), 1).astype(F32)

    def request(slot, _):
        row = 2.0 * cols[slot] - first_row
        hot = jnp.concatenate([jnp.where(row == row_lane, 1.0, 0.0), jnp.where(row + 1.0 == row_lane, 1.0, 0.0)], axis=0)
        pick_hot[pl.ds(pl.multiple_of(slot * 2 * NNZ, 2 * NNZ), 2 * NNZ)] = hot.astype(BF16)
        return 0

    lax.fori_loop(0, NB, request, 0)

    point_values.wait_recv()
    found = coefficients(end_sum(1))

    for n, (dx, dz) in enumerate(AROUND):
        xs, zs, shape, count = around_points[n]
        ok = inside(-dx, -dz)
        left = []
        for f in range(2):
            a = found[f]
            values = rseen[n, f:f + 1, :]
            for k in range(ITERS):
                values = values + a[k] * rseen[n, 2 * (k + 1) + f:2 * (k + 1) + f + 1, :]
            left.append((rec_hit[n, pl.ds(0, count)] * parts(values, ok)).astype(BF16))
        placed = lax.dot_general(jnp.concatenate(left, axis=0), rec_y[n], (((1,), (1,)), ((), ())),
                                 preferred_element_type=F32).reshape((2,) + shape + (NY,))
        v0[:, xs, zs, :] = placed - w[:, xs, zs, :]

    def own_residual(t, carry):
        for x in (HX + 2 * t, HX + 2 * t + 1):
            out = []
            for f in range(2):
                a = found[f]
                new = x0e[f, x, OWN_Z, :] + a[0] * v0[f, x, OWN_Z, :] + a[1] * v1[f, x, OWN_Z, :]
                new = new + a[2] * v2[f, x, OWN_Z, :]
                fwd[f, x - HX] = new
                u = cnte[x - HX] * new - obse[f, x - HX] - w[f, x, OWN_Z, :]
                v0[f, x, OWN_Z, :] = u
                p = u * u
                out.append(carry[f] + (p[0:8, 0:128] + p[8:16, 0:128]) + (p[0:8, 128:256] + p[8:16, 128:256]))
            carry = tuple(out)
        return carry

    squares = lax.fori_loop(0, CX // 2, own_residual, (jnp.zeros((8, 128), F32),) * 2)
    forward_store = pltpu.make_async_copy(fwd, fwd_out, out_sem.at[0])
    forward_store.start()

    sums = [squares] + krylov((2, 1))
    start_sum(2, pack_sums(sums))
    start_sum(3, end_sum(2))
    found_adjoint = coefficients(end_sum(3))

    def gradient_layer(x, _):
        total = jnp.zeros((CZ, NY), F32)
        for f in range(2):
            e = found_adjoint[f]
            own = a0e[f, x + HX, OWN_Z, :] + e[0] * v0[f, x + HX, OWN_Z, :] + e[1] * v1[f, x + HX, OWN_Z, :]
            own = own + e[2] * v2[f, x + HX, OWN_Z, :]
            total = total + LAPLACE_SHIFTS[f] * fwd[f, x] * own
        grad[pl.ds(pl.multiple_of(x * CZ, CZ), CZ)] = (-total).astype(BF16)
        return 0

    lax.fori_loop(0, CX, gradient_layer, 0)

    psend[...] = jnp.dot(pick_hot[...], grad[...], preferred_element_type=F32).astype(BF16).reshape(NB, 2 * NNZ, NY)

    for i, step in enumerate(LAYERS):
        back = ((4 - step[0]) % 4,) + step[1:]
        pltpu.make_async_remote_copy(
            src_ref=psend.at[i], dst_ref=precv.at[i], send_sem=pick_sem.at[0], recv_sem=pick_sem.at[1],
            device_id=beside(back), device_id_type=MESH).start()

    cov_load.wait()
    picks = pltpu.make_async_remote_copy(
        src_ref=precv, dst_ref=precv, send_sem=pick_sem.at[0], recv_sem=pick_sem.at[1],
        device_id=at(0, 1), device_id_type=MESH)
    picks.wait_recv()
    picked = psend[NB - 1].astype(F32) + jnp.sum(precv[...].astype(F32), axis=0)
    picked = picked.astype(BF16)

    term_row = iota((NNZ, BLOCK), 0)

    def term(t, total):
        for k in [8 * t + j for j in range(8)]:
            block = cov[k]
            made = lax.dot_general(picked[0:NNZ], block[:, 0:NY], (((1,), (1,)), ((), ())), preferred_element_type=F32)
            made += lax.dot_general(picked[NNZ:], block[:, NY:], (((1,), (1,)), ((), ())), preferred_element_type=F32)
            total = jnp.where(term_row == k, made, total)
        return total

    terms = lax.fori_loop(0, NNZ // 8, term, jnp.zeros((NNZ, BLOCK), F32))
    cov_rows = rows_v[0].astype(F32)
    out_row = iota((ROWS, NNZ), 0).astype(F32)
    total = grad[...].astype(F32)
    for half in range(2):
        hot = jnp.where(2.0 * cov_rows + float(half) == out_row, 1.0, 0.0)
        total = total + jnp.dot(hot, terms[:, half * NY:(half + 1) * NY], precision=lax.Precision.HIGHEST,
                                preferred_element_type=F32)
    pre[...] = total.reshape(CX, CZ, NY)
    pre_store = pltpu.make_async_copy(pre, pre_out, out_sem.at[1])
    pre_store.start()

    lists.wait_send()
    for copy in halos + adjoint_halos + [point_values]:
        copy.wait_send()
    pltpu.make_async_remote_copy(
        src_ref=cols.at[pl.ds(0, NB - 1)], dst_ref=cols.at[pl.ds(0, NB - 1)],
        send_sem=cols_sem.at[0], recv_sem=cols_sem.at[1],
        device_id=at(0, 1), device_id_type=MESH).wait_send()
    for stage in range(4):
        pltpu.make_async_remote_copy(
            src_ref=rsum.at[stage], dst_ref=rsum.at[stage],
            send_sem=sum_sem.at[stage, 0], recv_sem=sum_sem.at[stage, 1],
            device_id=at(0, 1), device_id_type=MESH).wait_send()
    picks.wait_send()
    forward_store.wait()
    pre_store.wait()


def hand_over(fwd_in, pre_in, fwd_out, pre_out):
    fwd_out[...] = fwd_in[...]
    pre_out[...] = pre_in[...]


def local(conductivity, initial_field, adjoint_initial, src_cell, src_amp, rec_cell, observed, cov_blocks, cov_rows, cov_cols):
    big = pltpu.VMEM((2, EX, EZ, NY), F32)
    one = pltpu.VMEM((EX, EZ, NY), F32)
    dma = pltpu.SemaphoreType.DMA
    scratch = [
        pltpu.VMEM(src_cell.shape, jnp.int32), pltpu.VMEM(src_amp.shape, F32),
        pltpu.VMEM(rec_cell.shape, jnp.int32), pltpu.VMEM(observed.shape, F32),
        pltpu.VMEM(cov_rows.shape, jnp.int32), pltpu.VMEM(cov_cols.shape, jnp.int32),
        pltpu.VMEM((32, 128), F32), pltpu.VMEM((NNZ, BLOCK, BLOCK), BF16),
        one, big, big, one, big,
        pltpu.VMEM((2, CX, CZ, NY), F32), pltpu.VMEM((CX, CZ, NY), F32),
        big, big, big, big,
        pltpu.VMEM((2, CX, CZ, NY), F32), pltpu.VMEM((ROWS, NY), BF16), pltpu.VMEM((CX, CZ, NY), F32),
        pltpu.VMEM((2 * NNZ * NB, ROWS), BF16),
    ]
    for count, slabs in ((2, 11), (2, 6), (4, 2), (2, 8), (2, 4), (4, 2)):
        scratch += [pltpu.VMEM((count, slabs, 16, NY), BF16)] * 2
    scratch += [
        pltpu.VMEM((8, 16, 128), F32), pltpu.VMEM((8, 128), F32), pltpu.VMEM((8, 8, 128), F32),
        pltpu.VMEM((8, 64, 128), F32), pltpu.VMEM((8, NY, 128), BF16), pltpu.VMEM((NB, NNZ, 128), F32),
        pltpu.VMEM((4, 8, 128), F32), pltpu.VMEM((4, NB - 1, 8, 128), F32),
        pltpu.VMEM((NB, 2 * NNZ, NY), BF16), pltpu.VMEM((NB - 1, 2 * NNZ, NY), BF16),
        dma((9,)), dma, dma((2,)), dma((2,)), dma((2,)), dma((8, 2)), dma((8, 2)), dma((2,)), dma((4, 2)), dma((2,)),
    ]
    anywhere = pl.BlockSpec(memory_space=pl.ANY)
    results = pl.pallas_call(
        kernel,
        out_shape=(
            jax.ShapeDtypeStruct((2, CX, CZ, NY), F32),
            jax.ShapeDtypeStruct((CX, CZ, NY), F32),
        ),
        in_specs=[anywhere] * 10,
        out_specs=(anywhere, anywhere),
        scratch_shapes=scratch,
        compiler_params=pltpu.CompilerParams(
            collective_id=0, has_side_effects=True, vmem_limit_bytes=56 * 2**20),
    )(conductivity, initial_field, adjoint_initial, src_cell, src_amp, rec_cell, observed,
      cov_blocks.reshape(NNZ, BLOCK, BLOCK), cov_rows, cov_cols)
    return pl.pallas_call(
        hand_over,
        out_shape=[jax.ShapeDtypeStruct(r.shape, r.dtype) for r in results],
    )(*results)


def solution(mesh):
    return jax.shard_map(
        local,
        mesh=mesh,
        in_specs=(
            P("brick", "depth", None),
            P(None, "brick", "depth", None),
            P(None, "brick", "depth", None),
            P("brick", "depth", None),
            P("brick", "depth", None, None),
            P("brick", "depth", None),
            P("brick", "depth", None, None),
            P("brick", "depth", None, None, None),
            P("brick", "depth", None),
            P("brick", "depth", None),
        ),
        out_specs=(P(None, "brick", "depth", None), P("brick", "depth", None)),
        check_vma=False,
    )
```

```python
import functools

import jax
import jax.numpy as jnp
from jax import lax
from jax.experimental import pallas as pl
from jax.experimental.pallas import tpu as pltpu
from jax.sharding import PartitionSpec as P

LAPLACE_SHIFTS = (0.5, 2.0)
CENTRE = (6.5, 8.0)
ITERS = 3
NB = 16
CX, CZ, NY = 8, 16, 256
HX, HZ = 6, 8
EX, EZ = CX + 2 * HX, CZ + 2 * HZ
NNZ, BLOCK = 16, 512
ROWS = CX * CZ
F32, BF16 = jnp.float32, jnp.bfloat16
MESH = pl.DeviceIdType.MESH
OWN_X, OWN_Z = pl.ds(HX, CX), pl.ds(HZ, CZ)

FACES_X = ((1, 0), (-1, 0))
FACES_Z = ((0, 1), (0, -1))
CORNERS = ((1, 1), (1, -1), (-1, 1), (-1, -1))
AROUND = FACES_X + FACES_Z + CORNERS

STEPS = sorted(
    ((i, j, k, c) for i in range(4) for j in range(4) for k in range(8) for c in range(2)),
    key=lambda s: -(8 * (min(s[0], 4 - s[0]) + min(s[1], 4 - s[1]) + min(s[2], 8 - s[2])) + s[3]))
PLANE = [s for s in STEPS if s[2:] == (0, 0) and s[:2] != (0, 0)]
COLUMN = [s for s in STEPS if s[:2] == (0, 0) and s[2:] != (0, 0)]
LAYERS = [s for s in STEPS if s[2] == 0 and s[1] % 2 == 0 and s != (0, 0, 0, 0)]


def iota(shape, dim):
    return lax.broadcasted_iota(jnp.int32, shape, dim)


def send_x(dx, width, skip=0):
    return pl.ds(HX + CX - skip - width, width) if dx > 0 else pl.ds(HX + skip, width)


def send_z(dz):
    return pl.ds(HZ + CZ - HZ, HZ) if dz > 0 else pl.ds(HZ, HZ)


def land_x(dx, width, skip=0):
    return pl.ds(HX - skip - width, width) if dx > 0 else pl.ds(HX + CX + skip, width)


def land_z(dz):
    return pl.ds(0, HZ) if dz > 0 else pl.ds(HZ + CZ, HZ)


def layer_at(dx, distance, land):
    if land:
        return HX - distance if dx > 0 else HX + CX + distance - 1
    return HX + CX - distance if dx > 0 else HX + distance - 1


def halves(first, second, dz):
    near = (iota((8, 1), 0) >= 4) if dz > 0 else (iota((8, 1), 0) < 4)
    return jnp.where(near, first, pltpu.roll(second, 4, 0))


def pack_face(field, dz):
    slabs = []
    for m in range(CX // 2):
        tiles = [halves(field[f][2 * m], field[f][2 * m + 1], dz) for f in range(2)]
        slabs.append(jnp.concatenate(tiles, axis=0).astype(BF16))
    return slabs


def pack_corner(field, near, zs, dz):
    tiles = [halves(field[f, near[0], zs, :], field[f, near[1], zs, :], dz) for f in range(2)]
    return tiles + [halves(field[0, near[2], zs, :], field[1, near[2], zs, :], dz)]


def cg_coefficients(nu, centre):
    def inner(p, q, shift):
        total = None
        for i, pi in enumerate(p):
            for j, qj in enumerate(q):
                term = pi * qj * nu[i + j + shift]
                total = term if total is None else total + term
        return total

    one = jnp.ones_like(nu[0])
    r, p = [one], [one]
    rr = nu[0]
    x = [jnp.zeros_like(one)] * ITERS
    for it in range(ITERS):
        step = rr / (inner(p, p, 1) + centre * inner(p, p, 0))
        for i, pi in enumerate(p):
            x[i] = x[i] + step * pi
        if it + 1 < ITERS:
            ap = [centre * pi for pi in p] + [jnp.zeros_like(one)]
            for i, pi in enumerate(p):
                ap[i + 1] = ap[i + 1] + pi
            r = r + [jnp.zeros_like(one)]
            r = [ri - step * ai for ri, ai in zip(r, ap)]
            new = inner(r, r, 0)
            beta = new / rr
            p = p + [jnp.zeros_like(one)]
            p = [ri + beta * pi for ri, pi in zip(r, p)]
            rr = new
    return x


def kernel(
    cond_in, x0_in, a0_in, src_in, amp_in, rec_in, obs_in, cov_in, rows_in, cols_in,
    fwd_out, pre_out,
    src_v, amp_v, rec_v, obs_v, rows_v, cols_v, aux, cov, ce, x0e, a0e, mask, srce, obse, cnte, v0, v1, v2, w, fwd, grad, pre, pick_hot,
    sx, rx, sz, rz, sc, rc, ax, bx, az, bz, ac, bc,
    rlist, seen, rseen, rec_hit, rec_y, cols, asum, rsum, psend, precv,
    in_sem, cov_sem, out_sem, list_sem, cols_sem, halo_sem, adj_sem, seen_sem, sum_sem, pick_sem,
):
    b, d = lax.axis_index("brick"), lax.axis_index("depth")

    def at(dx, dz):
        return lax.rem(b + dx + NB, NB), lax.rem(d + dz + NB, NB)

    barrier = pltpu.get_barrier_semaphore()
    for dx, dz in FACES_X + CORNERS:
        pl.semaphore_signal(barrier, inc=1, device_id=at(dx, dz), device_id_type=MESH)

    cx, cy = lax.div(d, 4), 2 * lax.rem(lax.div(d, 2), 2) + lax.div(b, 8)
    cz, core = lax.rem(b, 8), lax.rem(d, 2)

    def beside(step):
        x, y = lax.rem(cx + step[0], 4), lax.rem(cy + step[1], 4)
        return lax.rem(y, 2) * 8 + lax.rem(cz + step[2], 8), x * 4 + lax.div(y, 2) * 2 + lax.rem(core + step[3], 2)

    greeted = LAYERS + [s for s in PLANE if s[1] % 2] + [s for s in COLUMN if s[2]]
    for step in greeted:
        pl.semaphore_signal(barrier, inc=1, device_id=beside(step), device_id_type=MESH)

    loads = [
        pltpu.make_async_copy(x0_in, x0e.at[:, OWN_X, OWN_Z, :], in_sem.at[0]),
        pltpu.make_async_copy(cond_in, ce.at[OWN_X, OWN_Z, :], in_sem.at[1]),
        pltpu.make_async_copy(src_in, src_v, in_sem.at[2]),
        pltpu.make_async_copy(amp_in, amp_v, in_sem.at[3]),
        pltpu.make_async_copy(rec_in, rec_v, in_sem.at[4]),
        pltpu.make_async_copy(obs_in, obs_v, in_sem.at[5]),
        pltpu.make_async_copy(rows_in, rows_v, in_sem.at[6]),
        pltpu.make_async_copy(cols_in, cols_v, in_sem.at[7]),
        pltpu.make_async_copy(a0_in, a0e.at[:, OWN_X, OWN_Z, :], in_sem.at[8]),
    ]
    for load in loads:
        load.start()
    cov_load = pltpu.make_async_copy(cov_in, cov, cov_sem)
    cov_load.start()

    for load in loads[:2]:
        load.wait()
    for i, (dx, _) in enumerate(FACES_X):
        for f in range(2):
            sx[i, pl.ds(4 * f, 4)] = x0e[f, send_x(dx, 4), OWN_Z, :].astype(BF16)
        sx[i, pl.ds(8, 3)] = ce[send_x(dx, 3), OWN_Z, :].astype(BF16)
    for i, (_, dz) in enumerate(FACES_Z):
        zs = send_z(dz)
        for m, slab in enumerate(pack_face([x0e[f, OWN_X, zs, :] for f in range(2)], dz)):
            sz[i, m] = slab
        for m in range(2):
            tiles = [halves(ce[HX + k, zs, :], ce[HX + k + 1, zs, :], dz) for k in (4 * m, 4 * m + 2)]
            sz[i, 4 + m] = jnp.concatenate(tiles, axis=0).astype(BF16)
    for i, (dx, dz) in enumerate(CORNERS):
        zs = send_z(dz)
        near = [layer_at(dx, k, False) for k in (1, 2, 3)]
        tiles = pack_corner(x0e, near, zs, dz)
        tiles.append(halves(ce[near[0], zs, :], ce[near[1], zs, :], dz))
        sc[i, 0] = jnp.concatenate(tiles[:2], axis=0).astype(BF16)
        sc[i, 1] = jnp.concatenate(tiles[2:], axis=0).astype(BF16)

    for load in loads[2:8]:
        load.wait()

    def twice(row):
        return jnp.concatenate([row, row], axis=1)

    src_cell, rec_cell = src_v[0], rec_v[0]
    aux[0:1, :] = twice((src_cell >> 8).astype(F32))
    aux[1:2, :] = twice((src_cell & (NY - 1)).astype(F32))
    aux[2:4, :] = twice(amp_v[0, 0])
    aux[4:5, :] = twice((rec_cell >> 8).astype(F32))
    aux[5:6, :] = twice((rec_cell & (NY - 1)).astype(F32))
    aux[6:7, :] = jnp.where(iota((1, 128), 1) < 64, 1.0, 0.0)
    aux[7:9, :] = twice(obs_v[0, 0])
    aux[9:16, :] = jnp.zeros((7, 128), F32)
    col_row = jnp.where(iota((NNZ, NNZ), 0) == iota((NNZ, NNZ), 1), cols_v[0].astype(F32), 0.0)
    aux[16:32, :] = jnp.broadcast_to(jnp.sum(col_row, axis=1, keepdims=True), (NNZ, 128))

    pl.semaphore_wait(barrier, len(FACES_X) + len(CORNERS) + len(greeted))

    for n, (dx, dz) in enumerate(AROUND):
        pltpu.make_async_remote_copy(
            src_ref=aux.at[pl.ds(0, 16)], dst_ref=rlist.at[n], send_sem=list_sem.at[0], recv_sem=list_sem.at[1],
            device_id=at(dx, dz), device_id_type=MESH).start()

    def exchange(n, dx, dz, src, dst, sems):
        return pltpu.make_async_remote_copy(
            src_ref=src, dst_ref=dst, send_sem=sems.at[n, 0], recv_sem=sems.at[n, 1],
            device_id=at(dx, dz), device_id_type=MESH)

    halos = []
    for group, s, r in ((FACES_X, sx, rx), (FACES_Z, sz, rz), (CORNERS, sc, rc)):
        for i, (dx, dz) in enumerate(group):
            halos.append(exchange(len(halos), dx, dz, s.at[i], r.at[i], halo_sem))
    for copy in reversed(halos):
        copy.start()

    def inside(dx, dz):
        bx_, dz_ = b + dx, d + dz
        ok = (bx_ >= 0) & (bx_ < NB) & (dz_ >= 0) & (dz_ < NB)
        return jnp.where(ok, 1.0, 0.0).astype(F32)

    for i, (dx, dz) in enumerate(((0, 0),) + AROUND):
        xs = pl.ds(HX, CX) if dx == 0 else land_x(-dx, HX)
        zs = pl.ds(HZ, CZ) if dz == 0 else land_z(-dz)
        nx, nz = (CX if dx == 0 else HX), (CZ if dz == 0 else HZ)
        mask[xs, zs, :] = jnp.full((nx, nz, NY), inside(dx, dz), F32)

    for zs in (pl.ds(0, HZ), pl.ds(HZ + CZ, HZ)):
        for xs in (pl.ds(0, 3), pl.ds(EX - 3, 3)):
            x0e[:, xs, zs, :] = jnp.zeros((2, 3, HZ, NY), F32)
            a0e[:, xs, zs, :] = jnp.zeros((2, 3, HZ, NY), F32)
        for xs in (pl.ds(0, 4), pl.ds(EX - 4, 4)):
            ce[xs, zs, :] = jnp.zeros((4, HZ, NY), F32)

    lane = iota((1, 128), 1)

    def parts(row, ok):
        value = row * ok
        head = value.astype(BF16).astype(F32)
        return jnp.where(lane < 64, head, value - head)

    def where_points(table, base, dx, dz, width):
        xs = pl.ds(HX, CX) if dx == 0 else land_x(-dx, width)
        zs = pl.ds(HZ, CZ) if dz == 0 else land_z(-dz)
        nx, x_low = (CX, 0) if dx == 0 else ((width, 0) if dx > 0 else (width, CX - width))
        nz, z_low = (CZ, 0) if dz == 0 else ((HZ, 0) if dz > 0 else (HZ, CZ - HZ))
        shape = (nx, nz, 128)
        cell_row = ((iota(shape, 0) + x_low) * CZ + iota(shape, 1) + z_low).reshape(nx * nz, 128).astype(F32)
        hit = cell_row == table[base:base + 1, :]
        along_y = (iota((NY, 128), 0).astype(F32) == table[base + 1:base + 2, :]).astype(F32).astype(BF16)
        return hit, along_y, xs, zs, (nx, nz)

    def place(hit, along_y, rows, shape):
        left = jnp.concatenate([jnp.where(hit, row, 0.0).astype(BF16) for row in rows], axis=0)
        placed = lax.dot_general(left, along_y, (((1,), (1,)), ((), ())), preferred_element_type=F32)
        return placed.reshape((len(rows),) + shape + (NY,))

    def place_sources(table, dx, dz):
        ok = inside(dx, dz)
        hit, along_y, xs, zs, shape = where_points(table, 0, dx, dz, 3)
        srce[:, xs, zs, :] = place(hit, along_y, [parts(table[2 + f:3 + f, :], ok) for f in range(2)], shape)

    def place_own_receivers():
        rows = [own_table[6:7, :]] + [parts(own_table[7 + f:8 + f, :], 1.0) for f in range(2)]
        placed = place(*own_points[:2], rows, own_points[4])
        cnte[...] = placed[0]
        obse[...] = placed[1:3]

    own_table = aux[0:16, :]
    place_sources(own_table, 0, 0)

    loads[8].wait()
    for i, (dx, _) in enumerate(FACES_X):
        for f in range(2):
            ax[i, pl.ds(4 * f, 4)] = a0e[f, send_x(dx, 4), OWN_Z, :].astype(BF16)
    for i, (_, dz) in enumerate(FACES_Z):
        for m, slab in enumerate(pack_face([a0e[f, OWN_X, send_z(dz), :] for f in range(2)], dz)):
            az[i, m] = slab
    for i, (dx, dz) in enumerate(CORNERS):
        tiles = pack_corner(a0e, [layer_at(dx, k, False) for k in (1, 2, 3)], send_z(dz), dz)
        ac[i, 0] = jnp.concatenate(tiles[:2], axis=0).astype(BF16)
        ac[i, 1] = jnp.concatenate([tiles[2], tiles[2]], axis=0).astype(BF16)
    adjoint_halos = []
    for group, s, r in ((FACES_X, ax, bx), (FACES_Z, az, bz), (CORNERS, ac, bc)):
        for i, (dx, dz) in enumerate(group):
            adjoint_halos.append(exchange(len(adjoint_halos), dx, dz, s.at[i], r.at[i], adj_sem))

    lists = pltpu.make_async_remote_copy(
        src_ref=rlist, dst_ref=rlist, send_sem=list_sem.at[0], recv_sem=list_sem.at[1],
        device_id=at(1, 0), device_id_type=MESH)
    lists.wait_recv()
    for n, (dx, dz) in enumerate(AROUND):
        place_sources(rlist[n], -dx, -dz)
    for copy in adjoint_halos:
        copy.start()

    def unpack_face(message, field, zs, ok):
        for m in range(CX // 2):
            slab = message[m].astype(F32) * ok
            for f in range(2):
                tile = slab[8 * f:8 * f + 8]
                field[f, HX + 2 * m, zs, :] = tile
                field[f, HX + 2 * m + 1, zs, :] = pltpu.roll(tile, 4, 0)

    def unpack_corner(message, field, near, zs, ok):
        first, second = message[0].astype(F32) * ok, message[1].astype(F32)
        for f in range(2):
            tile = first[8 * f:8 * f + 8]
            field[f, near[0], zs, :] = tile
            field[f, near[1], zs, :] = pltpu.roll(tile, 4, 0)
        tile = second[0:8] * ok
        field[0, near[2], zs, :] = tile
        field[1, near[2], zs, :] = pltpu.roll(tile, 4, 0)
        return second[8:16]

    for n, (dx, dz) in enumerate(AROUND):
        halos[n].wait_recv()
        ok = inside(-dx, -dz)
        if dz == 0:
            for f in range(2):
                x0e[f, land_x(dx, 4), OWN_Z, :] = rx[n, pl.ds(4 * f, 4)].astype(F32) * ok
            ce[land_x(dx, 3), OWN_Z, :] = rx[n, pl.ds(8, 3)].astype(F32)
        elif dx == 0:
            unpack_face(rz.at[n - 2], x0e, land_z(dz), ok)
            for m in range(2):
                slab = rz[n - 2, 4 + m].astype(F32)
                for k in range(2):
                    tile = slab[8 * k:8 * k + 8]
                    ce[HX + 4 * m + 2 * k, land_z(dz), :] = tile
                    ce[HX + 4 * m + 2 * k + 1, land_z(dz), :] = pltpu.roll(tile, 4, 0)
        else:
            near = [layer_at(dx, k, True) for k in (1, 2, 3)]
            second = unpack_corner(rc.at[n - 4], x0e, near, land_z(dz), ok)
            ce[near[0], land_z(dz), :] = second
            ce[near[1], land_z(dz), :] = pltpu.roll(second, 4, 0)

    lane_row = iota((1, 128), 1)

    def around(ref, f, x):
        c = ref[f, x]
        total = ref[f, x - 1] + ref[f, x + 1]
        total = total + pltpu.roll(c, 1, 0) + pltpu.roll(c, EZ - 1, 0)
        up, down = pltpu.roll(c, 1, 1), pltpu.roll(c, NY - 1, 1)
        low = jnp.where(lane_row == 0, 0.0, up[:, 0:128]) + down[:, 0:128]
        high = up[:, 128:] + jnp.where(lane_row == 127, 0.0, down[:, 128:])
        return c, total + jnp.concatenate([low, high], axis=1)

    def fold(first, second):
        p = first[HZ:HZ + CZ] * second[HZ:HZ + CZ]
        return (p[0:8, 0:128] + p[8:16, 0:128]) + (p[0:8, 128:256] + p[8:16, 128:256])

    def residual_layer(x):
        made = []
        for f in range(2):
            c, total = around(x0e, f, x)
            diag = 6.0 + LAPLACE_SHIFTS[f] * ce[x]
            r = (srce[f, x] - (diag * c - total)) * mask[x]
            v0[f, x] = r
            made.append((r, r))
        return made

    def apply_layer(src, dst):
        def run(x):
            made = []
            for f in range(2):
                c, total = around(src, f, x)
                diag = (6.0 - CENTRE[f]) + LAPLACE_SHIFTS[f] * ce[x]
                new = (diag * c - total) * mask[x]
                if dst is not None:
                    dst[f, x] = new
                made.append((c, new))
            return made
        return run

    def sweep(layer, width, want):
        def outer(t, _):
            layer(HX - 1 - t)
            layer(HX + CX + t)
            return 0

        def summed(t, carry):
            for x in [HX + 8 * t + j for j in range(8)]:
                sums = []
                for c, new in layer(x):
                    for which in want:
                        sums.append(fold(c, new) if which == "cross" else fold(new, new))
                carry = tuple(s + t for s, t in zip(carry, sums))
            return carry

        zero = tuple(jnp.zeros((8, 128), F32) for _ in range(2 * len(want)))
        out = lax.fori_loop(0, CX // 8, summed, zero)
        if width:
            for t in range(width):
                outer(t, 0)
        half = len(want)
        return [(out[i], out[half + i]) for i in range(half)]

    def krylov(widths):
        sums = sweep(apply_layer(v0, v1), widths[0], ("cross", "square"))
        sums += sweep(apply_layer(v1, v2), widths[1], ("cross", "square"))
        sums += sweep(apply_layer(v2, None), 0, ("cross",))
        return sums

    low_lanes = iota((8, 128), 1) < 64
    sub = iota((8, 128), 0)

    def start_sum(stage, value):
        asum[stage] = value
        for i, step in enumerate(PLANE if stage % 2 else COLUMN):
            pltpu.make_async_remote_copy(
                src_ref=asum.at[stage], dst_ref=rsum.at[stage, i],
                send_sem=sum_sem.at[stage, 0], recv_sem=sum_sem.at[stage, 1],
                device_id=beside(step), device_id_type=MESH).start()

    def end_sum(stage):
        everything = pltpu.make_async_remote_copy(
            src_ref=rsum.at[stage], dst_ref=rsum.at[stage],
            send_sem=sum_sem.at[stage, 0], recv_sem=sum_sem.at[stage, 1],
            device_id=at(0, 1), device_id_type=MESH)
        everything.wait_recv()
        return asum[stage] + jnp.sum(rsum[stage], axis=0)

    def pack_sums(sums):
        tile = jnp.zeros((8, 128), F32)
        for k, (s0, s1) in enumerate(sums):
            both = jnp.where(low_lanes, s0 + pltpu.roll(s0, 64, 1), s1 + pltpu.roll(s1, 64, 1))
            tile = jnp.where(sub == k, jnp.sum(both, axis=0, keepdims=True), tile)
        return tile

    def coefficients(tile):
        found = []
        for f in range(2):
            keep = low_lanes if f == 0 else jnp.logical_not(low_lanes)
            column = jnp.sum(jnp.where(keep, tile, 0.0), axis=1, keepdims=True)
            nu = [column[k:k + 1, :] for k in range(2 * ITERS)]
            found.append(cg_coefficients(nu, CENTRE[f]))
        return found

    sums = sweep(residual_layer, 3, ("square",))
    sums += krylov((2, 1))
    start_sum(0, pack_sums(sums))

    for i, step in enumerate(LAYERS):
        pltpu.make_async_remote_copy(
            src_ref=aux.at[pl.ds(16, 16)], dst_ref=cols.at[i], send_sem=cols_sem.at[0], recv_sem=cols_sem.at[1],
            device_id=beside(step), device_id_type=MESH).start()

    own_points = where_points(own_table, 4, 0, 0, 0)
    place_own_receivers()
    here = jnp.where(own_points[0], 1.0, 0.0)
    fields = []
    for ref in (x0e, v0, v1, v2):
        for f in range(2):
            fields.append(ref[f, OWN_X, OWN_Z, :].reshape(ROWS, NY))
    fields = jnp.concatenate(fields, axis=0)
    head = fields.astype(BF16)
    tail = (fields - head.astype(F32)).astype(BF16)
    columns = lax.dot_general(head, own_points[1], (((1,), (0,)), ((), ())), preferred_element_type=F32)
    columns += lax.dot_general(tail, own_points[1], (((1,), (0,)), ((), ())), preferred_element_type=F32)
    for j in range(8):
        row = jnp.sum(columns[ROWS * j:ROWS * (j + 1)] * here, axis=0, keepdims=True)
        seen[j:j + 1, :] = row - own_table[7 + j:8 + j, :] if j < 2 else row
    for n, (dx, dz) in enumerate(AROUND):
        pltpu.make_async_remote_copy(
            src_ref=seen, dst_ref=rseen.at[n], send_sem=seen_sem.at[0], recv_sem=seen_sem.at[1],
            device_id=at(dx, dz), device_id_type=MESH).start()
    point_values = pltpu.make_async_remote_copy(
        src_ref=rseen, dst_ref=rseen, send_sem=seen_sem.at[0], recv_sem=seen_sem.at[1],
        device_id=at(1, 0), device_id_type=MESH)
    around_points = []
    for n, (dx, dz) in enumerate(AROUND):
        hit, along_y, xs, zs, shape = where_points(rlist[n], 4, -dx, -dz, 3)
        rec_y[n] = along_y
        count = shape[0] * shape[1]
        rec_hit[n, pl.ds(0, count)] = jnp.where(hit, 1.0, 0.0)
        around_points.append((xs, zs, shape, count))
    for n, (dx, dz) in enumerate(AROUND):
        adjoint_halos[n].wait_recv()
        ok = inside(-dx, -dz)
        if dz == 0:
            for f in range(2):
                a0e[f, land_x(dx, 4), OWN_Z, :] = bx[n, pl.ds(4 * f, 4)].astype(F32) * ok
        elif dx == 0:
            unpack_face(bz.at[n - 2], a0e, land_z(dz), ok)
        else:
            unpack_corner(bc.at[n - 4], a0e, [layer_at(dx, k, True) for k in (1, 2, 3)], land_z(dz), ok)

    start_sum(1, end_sum(0))

    def adjoint_part(t, _):
        for x in (HX - 3 + 2 * t, HX - 2 + 2 * t):
            for f in range(2):
                c, total = around(a0e, f, x)
                diag = 6.0 + LAPLACE_SHIFTS[f] * ce[x]
                w[f, x] = (diag * c - total) * mask[x]
        return 0

    lax.fori_loop(0, CX // 2 + 3, adjoint_part, 0)

    pltpu.make_async_remote_copy(
        src_ref=cols.at[pl.ds(0, NB - 1)], dst_ref=cols.at[pl.ds(0, NB - 1)],
        send_sem=cols_sem.at[0], recv_sem=cols_sem.at[1],
        device_id=at(0, 1), device_id_type=MESH).wait_recv()
    cols[NB - 1] = aux[16:32, :]
    first_row = (d * ROWS).astype(F32)
    row_lane = iota((NNZ, 128), 1).astype(F32)

    def request(slot, _):
        row = 2.0 * cols[slot] - first_row
        hot = jnp.concatenate([jnp.where(row == row_lane, 1.0, 0.0), jnp.where(row + 1.0 == row_lane, 1.0, 0.0)], axis=0)
        pick_hot[pl.ds(pl.multiple_of(slot * 2 * NNZ, 2 * NNZ), 2 * NNZ)] = hot.astype(BF16)
        return 0

    lax.fori_loop(0, NB, request, 0)

    point_values.wait_recv()
    found = coefficients(end_sum(1))

    for n, (dx, dz) in enumerate(AROUND):
        xs, zs, shape, count = around_points[n]
        ok = inside(-dx, -dz)
        left = []
        for f in range(2):
            a = found[f]
            values = rseen[n, f:f + 1, :]
            for k in range(ITERS):
                values = values + a[k] * rseen[n, 2 * (k + 1) + f:2 * (k + 1) + f + 1, :]
            left.append((rec_hit[n, pl.ds(0, count)] * parts(values, ok)).astype(BF16))
        placed = lax.dot_general(jnp.concatenate(left, axis=0), rec_y[n], (((1,), (1,)), ((), ())),
                                 preferred_element_type=F32).reshape((2,) + shape + (NY,))
        v0[:, xs, zs, :] = placed - w[:, xs, zs, :]

    def own_residual(t, carry):
        for x in [HX + 8 * t + j for j in range(8)]:
            out = []
            for f in range(2):
                a = found[f]
                new = x0e[f, x, OWN_Z, :] + a[0] * v0[f, x, OWN_Z, :] + a[1] * v1[f, x, OWN_Z, :]
                new = new + a[2] * v2[f, x, OWN_Z, :]
                fwd[f, x - HX] = new
                u = cnte[x - HX] * new - obse[f, x - HX] - w[f, x, OWN_Z, :]
                v0[f, x, OWN_Z, :] = u
                p = u * u
                out.append(carry[f] + (p[0:8, 0:128] + p[8:16, 0:128]) + (p[0:8, 128:256] + p[8:16, 128:256]))
            carry = tuple(out)
        return carry

    squares = lax.fori_loop(0, CX // 8, own_residual, (jnp.zeros((8, 128), F32),) * 2)
    forward_store = pltpu.make_async_copy(fwd, fwd_out, out_sem.at[0])
    forward_store.start()

    sums = [squares] + krylov((2, 1))
    start_sum(2, pack_sums(sums))
    start_sum(3, end_sum(2))
    found_adjoint = coefficients(end_sum(3))

    def gradient_layer(x, _):
        total = jnp.zeros((CZ, NY), F32)
        for f in range(2):
            e = found_adjoint[f]
            own = a0e[f, x + HX, OWN_Z, :] + e[0] * v0[f, x + HX, OWN_Z, :] + e[1] * v1[f, x + HX, OWN_Z, :]
            own = own + e[2] * v2[f, x + HX, OWN_Z, :]
            total = total + LAPLACE_SHIFTS[f] * fwd[f, x] * own
        grad[pl.ds(x * CZ, CZ)] = (-total).astype(BF16)
        return 0

    for x in range(CX):
        gradient_layer(x, 0)

    psend[...] = jnp.dot(pick_hot[...], grad[...], preferred_element_type=F32).astype(BF16).reshape(NB, 2 * NNZ, NY)

    for i, step in enumerate(LAYERS):
        back = ((4 - step[0]) % 4,) + step[1:]
        pltpu.make_async_remote_copy(
            src_ref=psend.at[i], dst_ref=precv.at[i], send_sem=pick_sem.at[0], recv_sem=pick_sem.at[1],
            device_id=beside(back), device_id_type=MESH).start()

    cov_load.wait()
    picks = pltpu.make_async_remote_copy(
        src_ref=precv, dst_ref=precv, send_sem=pick_sem.at[0], recv_sem=pick_sem.at[1],
        device_id=at(0, 1), device_id_type=MESH)
    picks.wait_recv()
    picked = psend[NB - 1].astype(F32) + jnp.sum(precv[...].astype(F32), axis=0)
    picked = picked.astype(BF16)

    term_row = iota((NNZ, BLOCK), 0)

    def term(t, total):
        for k in range(NNZ):
            block = cov[k]
            made = lax.dot_general(picked[0:NNZ], block[:, 0:NY], (((1,), (1,)), ((), ())), preferred_element_type=F32)
            made += lax.dot_general(picked[NNZ:], block[:, NY:], (((1,), (1,)), ((), ())), preferred_element_type=F32)
            total = jnp.where(term_row == k, made, total)
        return total

    terms = lax.fori_loop(0, 1, term, jnp.zeros((NNZ, BLOCK), F32))
    cov_rows = rows_v[0].astype(F32)
    out_row = iota((ROWS, NNZ), 0).astype(F32)
    total = grad[...].astype(F32)
    for half in range(2):
        hot = jnp.where(2.0 * cov_rows + float(half) == out_row, 1.0, 0.0)
        total = total + jnp.dot(hot, terms[:, half * NY:(half + 1) * NY], precision=lax.Precision.HIGHEST,
                                preferred_element_type=F32)
    pre[...] = total.reshape(CX, CZ, NY)
    pre_store = pltpu.make_async_copy(pre, pre_out, out_sem.at[1])
    pre_store.start()

    lists.wait_send()
    for copy in halos + adjoint_halos + [point_values]:
        copy.wait_send()
    pltpu.make_async_remote_copy(
        src_ref=cols.at[pl.ds(0, NB - 1)], dst_ref=cols.at[pl.ds(0, NB - 1)],
        send_sem=cols_sem.at[0], recv_sem=cols_sem.at[1],
        device_id=at(0, 1), device_id_type=MESH).wait_send()
    for stage in range(4):
        pltpu.make_async_remote_copy(
            src_ref=rsum.at[stage], dst_ref=rsum.at[stage],
            send_sem=sum_sem.at[stage, 0], recv_sem=sum_sem.at[stage, 1],
            device_id=at(0, 1), device_id_type=MESH).wait_send()
    picks.wait_send()
    forward_store.wait()
    pre_store.wait()


def hand_over(fwd_in, pre_in, fwd_out, pre_out):
    fwd_out[...] = fwd_in[...]
    pre_out[...] = pre_in[...]


def local(conductivity, initial_field, adjoint_initial, src_cell, src_amp, rec_cell, observed, cov_blocks, cov_rows, cov_cols):
    big = pltpu.VMEM((2, EX, EZ, NY), F32)
    one = pltpu.VMEM((EX, EZ, NY), F32)
    dma = pltpu.SemaphoreType.DMA
    scratch = [
        pltpu.VMEM(src_cell.shape, jnp.int32), pltpu.VMEM(src_amp.shape, F32),
        pltpu.VMEM(rec_cell.shape, jnp.int32), pltpu.VMEM(observed.shape, F32),
        pltpu.VMEM(cov_rows.shape, jnp.int32), pltpu.VMEM(cov_cols.shape, jnp.int32),
        pltpu.VMEM((32, 128), F32), pltpu.VMEM((NNZ, BLOCK, BLOCK), BF16),
        one, big, big, one, big,
        pltpu.VMEM((2, CX, CZ, NY), F32), pltpu.VMEM((CX, CZ, NY), F32),
        big, big, big, big,
        pltpu.VMEM((2, CX, CZ, NY), F32), pltpu.VMEM((ROWS, NY), BF16), pltpu.VMEM((CX, CZ, NY), F32),
        pltpu.VMEM((2 * NNZ * NB, ROWS), BF16),
    ]
    for count, slabs in ((2, 11), (2, 6), (4, 2), (2, 8), (2, 4), (4, 2)):
        scratch += [pltpu.VMEM((count, slabs, 16, NY), BF16)] * 2
    scratch += [
        pltpu.VMEM((8, 16, 128), F32), pltpu.VMEM((8, 128), F32), pltpu.VMEM((8, 8, 128), F32),
        pltpu.VMEM((8, 64, 128), F32), pltpu.VMEM((8, NY, 128), BF16), pltpu.VMEM((NB, NNZ, 128), F32),
        pltpu.VMEM((4, 8, 128), F32), pltpu.VMEM((4, NB - 1, 8, 128), F32),
        pltpu.VMEM((NB, 2 * NNZ, NY), BF16), pltpu.VMEM((NB - 1, 2 * NNZ, NY), BF16),
        dma((9,)), dma, dma((2,)), dma((2,)), dma((2,)), dma((8, 2)), dma((8, 2)), dma((2,)), dma((4, 2)), dma((2,)),
    ]
    anywhere = pl.BlockSpec(memory_space=pl.ANY)
    results = pl.pallas_call(
        kernel,
        out_shape=(
            jax.ShapeDtypeStruct((2, CX, CZ, NY), F32),
            jax.ShapeDtypeStruct((CX, CZ, NY), F32),
        ),
        in_specs=[anywhere] * 10,
        out_specs=(anywhere, anywhere),
        scratch_shapes=scratch,
        compiler_params=pltpu.CompilerParams(
            collective_id=0, has_side_effects=True, vmem_limit_bytes=56 * 2**20),
    )(conductivity, initial_field, adjoint_initial, src_cell, src_amp, rec_cell, observed,
      cov_blocks.reshape(NNZ, BLOCK, BLOCK), cov_rows, cov_cols)
    return pl.pallas_call(
        hand_over,
        out_shape=[jax.ShapeDtypeStruct(r.shape, r.dtype) for r in results],
    )(*results)


def solution(mesh):
    return jax.shard_map(
        local,
        mesh=mesh,
        in_specs=(
            P("brick", "depth", None),
            P(None, "brick", "depth", None),
            P(None, "brick", "depth", None),
            P("brick", "depth", None),
            P("brick", "depth", None, None),
            P("brick", "depth", None),
            P("brick", "depth", None, None),
            P("brick", "depth", None, None, None),
            P("brick", "depth", None),
            P("brick", "depth", None),
        ),
        out_specs=(P(None, "brick", "depth", None), P("brick", "depth", None)),
        check_vma=False,
    )
```

```python
import functools

import jax
import jax.numpy as jnp
from jax import lax
from jax.experimental import pallas as pl
from jax.experimental.pallas import tpu as pltpu
from jax.sharding import PartitionSpec as P

LAPLACE_SHIFTS = (0.5, 2.0)
CENTRE = (6.5, 8.0)
ITERS = 3
NB = 16
CX, CZ, NY = 8, 16, 256
HX, HZ = 6, 8
EX, EZ = CX + 2 * HX, CZ + 2 * HZ
NNZ, BLOCK = 16, 512
ROWS = CX * CZ
F32, BF16 = jnp.float32, jnp.bfloat16
MESH = pl.DeviceIdType.MESH
OWN_X, OWN_Z = pl.ds(HX, CX), pl.ds(HZ, CZ)

FACES_X = ((1, 0), (-1, 0))
FACES_Z = ((0, 1), (0, -1))
CORNERS = ((1, 1), (1, -1), (-1, 1), (-1, -1))
AROUND = FACES_X + FACES_Z + CORNERS

STEPS = sorted(
    ((i, j, k, c) for i in range(4) for j in range(4) for k in range(8) for c in range(2)),
    key=lambda s: -(8 * (min(s[0], 4 - s[0]) + min(s[1], 4 - s[1]) + min(s[2], 8 - s[2])) + s[3]))
PLANE = [s for s in STEPS if s[2:] == (0, 0) and s[:2] != (0, 0)]
COLUMN = [s for s in STEPS if s[:2] == (0, 0) and s[2:] != (0, 0)]
LAYERS = [s for s in STEPS if s[2] == 0 and s[1] % 2 == 0 and s != (0, 0, 0, 0)]


def iota(shape, dim):
    return lax.broadcasted_iota(jnp.int32, shape, dim)


def send_x(dx, width, skip=0):
    return pl.ds(HX + CX - skip - width, width) if dx > 0 else pl.ds(HX + skip, width)


def send_z(dz):
    return pl.ds(HZ + CZ - HZ, HZ) if dz > 0 else pl.ds(HZ, HZ)


def land_x(dx, width, skip=0):
    return pl.ds(HX - skip - width, width) if dx > 0 else pl.ds(HX + CX + skip, width)


def land_z(dz):
    return pl.ds(0, HZ) if dz > 0 else pl.ds(HZ + CZ, HZ)


def layer_at(dx, distance, land):
    if land:
        return HX - distance if dx > 0 else HX + CX + distance - 1
    return HX + CX - distance if dx > 0 else HX + distance - 1


def halves(first, second, dz):
    near = (iota((8, 1), 0) >= 4) if dz > 0 else (iota((8, 1), 0) < 4)
    return jnp.where(near, first, pltpu.roll(second, 4, 0))


def pack_face(field, dz):
    slabs = []
    for m in range(CX // 2):
        tiles = [halves(field[f][2 * m], field[f][2 * m + 1], dz) for f in range(2)]
        slabs.append(jnp.concatenate(tiles, axis=0).astype(BF16))
    return slabs


def pack_corner(field, near, zs, dz):
    tiles = [halves(field[f, near[0], zs, :], field[f, near[1], zs, :], dz) for f in range(2)]
    return tiles + [halves(field[0, near[2], zs, :], field[1, near[2], zs, :], dz)]


def cg_coefficients(nu, centre):
    def inner(p, q, shift):
        total = None
        for i, pi in enumerate(p):
            for j, qj in enumerate(q):
                term = pi * qj * nu[i + j + shift]
                total = term if total is None else total + term
        return total

    one = jnp.ones_like(nu[0])
    r, p = [one], [one]
    rr = nu[0]
    x = [jnp.zeros_like(one)] * ITERS
    for it in range(ITERS):
        step = rr / (inner(p, p, 1) + centre * inner(p, p, 0))
        for i, pi in enumerate(p):
            x[i] = x[i] + step * pi
        if it + 1 < ITERS:
            ap = [centre * pi for pi in p] + [jnp.zeros_like(one)]
            for i, pi in enumerate(p):
                ap[i + 1] = ap[i + 1] + pi
            r = r + [jnp.zeros_like(one)]
            r = [ri - step * ai for ri, ai in zip(r, ap)]
            new = inner(r, r, 0)
            beta = new / rr
            p = p + [jnp.zeros_like(one)]
            p = [ri + beta * pi for ri, pi in zip(r, p)]
            rr = new
    return x


def kernel(
    cond_in, x0_in, a0_in, src_in, amp_in, rec_in, obs_in, cov_in, rows_in, cols_in,
    fwd_out, pre_out,
    src_v, amp_v, rec_v, obs_v, rows_v, cols_v, aux, cov, ce, x0e, a0e, mask, srce, obse, cnte, v0, v1, v2, w, fwd, grad, pre, pick_hot,
    sx, rx, sz, rz, sc, rc, ax, bx, az, bz, ac, bc,
    rlist, seen, rseen, rec_hit, rec_y, cols, asum, rsum, psend, precv,
    in_sem, cov_sem, out_sem, list_sem, cols_sem, halo_sem, adj_sem, seen_sem, sum_sem, pick_sem,
):
    b, d = lax.axis_index("brick"), lax.axis_index("depth")

    def at(dx, dz):
        return lax.rem(b + dx + NB, NB), lax.rem(d + dz + NB, NB)

    barrier = pltpu.get_barrier_semaphore()
    for dx, dz in FACES_X + CORNERS:
        pl.semaphore_signal(barrier, inc=1, device_id=at(dx, dz), device_id_type=MESH)

    cx, cy = lax.div(d, 4), 2 * lax.rem(lax.div(d, 2), 2) + lax.div(b, 8)
    cz, core = lax.rem(b, 8), lax.rem(d, 2)

    def beside(step):
        x, y = lax.rem(cx + step[0], 4), lax.rem(cy + step[1], 4)
        return lax.rem(y, 2) * 8 + lax.rem(cz + step[2], 8), x * 4 + lax.div(y, 2) * 2 + lax.rem(core + step[3], 2)

    greeted = LAYERS + [s for s in PLANE if s[1] % 2] + [s for s in COLUMN if s[2]]
    for step in greeted:
        pl.semaphore_signal(barrier, inc=1, device_id=beside(step), device_id_type=MESH)

    loads = [
        pltpu.make_async_copy(x0_in, x0e.at[:, OWN_X, OWN_Z, :], in_sem.at[0]),
        pltpu.make_async_copy(cond_in, ce.at[OWN_X, OWN_Z, :], in_sem.at[1]),
        pltpu.make_async_copy(src_in, src_v, in_sem.at[2]),
        pltpu.make_async_copy(amp_in, amp_v, in_sem.at[3]),
        pltpu.make_async_copy(rec_in, rec_v, in_sem.at[4]),
        pltpu.make_async_copy(obs_in, obs_v, in_sem.at[5]),
        pltpu.make_async_copy(rows_in, rows_v, in_sem.at[6]),
        pltpu.make_async_copy(cols_in, cols_v, in_sem.at[7]),
        pltpu.make_async_copy(a0_in, a0e.at[:, OWN_X, OWN_Z, :], in_sem.at[8]),
    ]
    for load in loads:
        load.start()
    cov_load = pltpu.make_async_copy(cov_in, cov, cov_sem)
    cov_load.start()

    for load in loads[:2]:
        load.wait()
    for i, (dx, _) in enumerate(FACES_X):
        for f in range(2):
            sx[i, pl.ds(4 * f, 4)] = x0e[f, send_x(dx, 4), OWN_Z, :].astype(BF16)
        sx[i, pl.ds(8, 3)] = ce[send_x(dx, 3), OWN_Z, :].astype(BF16)
    for i, (_, dz) in enumerate(FACES_Z):
        zs = send_z(dz)
        for m, slab in enumerate(pack_face([x0e[f, OWN_X, zs, :] for f in range(2)], dz)):
            sz[i, m] = slab
        for m in range(2):
            tiles = [halves(ce[HX + k, zs, :], ce[HX + k + 1, zs, :], dz) for k in (4 * m, 4 * m + 2)]
            sz[i, 4 + m] = jnp.concatenate(tiles, axis=0).astype(BF16)
    for i, (dx, dz) in enumerate(CORNERS):
        zs = send_z(dz)
        near = [layer_at(dx, k, False) for k in (1, 2, 3)]
        tiles = pack_corner(x0e, near, zs, dz)
        tiles.append(halves(ce[near[0], zs, :], ce[near[1], zs, :], dz))
        sc[i, 0] = jnp.concatenate(tiles[:2], axis=0).astype(BF16)
        sc[i, 1] = jnp.concatenate(tiles[2:], axis=0).astype(BF16)

    for load in loads[2:8]:
        load.wait()

    def twice(row):
        return jnp.concatenate([row, row], axis=1)

    src_cell, rec_cell = src_v[0], rec_v[0]
    aux[0:1, :] = twice((src_cell >> 8).astype(F32))
    aux[1:2, :] = twice((src_cell & (NY - 1)).astype(F32))
    aux[2:4, :] = twice(amp_v[0, 0])
    aux[4:5, :] = twice((rec_cell >> 8).astype(F32))
    aux[5:6, :] = twice((rec_cell & (NY - 1)).astype(F32))
    aux[6:7, :] = jnp.where(iota((1, 128), 1) < 64, 1.0, 0.0)
    aux[7:9, :] = twice(obs_v[0, 0])
    aux[9:16, :] = jnp.zeros((7, 128), F32)
    col_row = jnp.where(iota((NNZ, NNZ), 0) == iota((NNZ, NNZ), 1), cols_v[0].astype(F32), 0.0)
    aux[16:32, :] = jnp.broadcast_to(jnp.sum(col_row, axis=1, keepdims=True), (NNZ, 128))

    pl.semaphore_wait(barrier, len(FACES_X) + len(CORNERS) + len(greeted))

    def exchange(n, dx, dz, src, dst, sems):
        return pltpu.make_async_remote_copy(
            src_ref=src, dst_ref=dst, send_sem=sems.at[n, 0], recv_sem=sems.at[n, 1],
            device_id=at(dx, dz), device_id_type=MESH)

    halos = []
    for group, s, r in ((FACES_X, sx, rx), (FACES_Z, sz, rz), (CORNERS, sc, rc)):
        for i, (dx, dz) in enumerate(group):
            halos.append(exchange(len(halos), dx, dz, s.at[i], r.at[i], halo_sem))
    for copy in reversed(halos):
        copy.start()
    for n, (dx, dz) in enumerate(AROUND):
        pltpu.make_async_remote_copy(
            src_ref=aux.at[pl.ds(0, 16)], dst_ref=rlist.at[n], send_sem=list_sem.at[0], recv_sem=list_sem.at[1],
            device_id=at(dx, dz), device_id_type=MESH).start()


    def inside(dx, dz):
        bx_, dz_ = b + dx, d + dz
        ok = (bx_ >= 0) & (bx_ < NB) & (dz_ >= 0) & (dz_ < NB)
        return jnp.where(ok, 1.0, 0.0).astype(F32)

    for i, (dx, dz) in enumerate(((0, 0),) + AROUND):
        xs = pl.ds(HX, CX) if dx == 0 else land_x(-dx, HX)
        zs = pl.ds(HZ, CZ) if dz == 0 else land_z(-dz)
        nx, nz = (CX if dx == 0 else HX), (CZ if dz == 0 else HZ)
        mask[xs, zs, :] = jnp.full((nx, nz, NY), inside(dx, dz), F32)

    for zs in (pl.ds(0, HZ), pl.ds(HZ + CZ, HZ)):
        for xs in (pl.ds(0, 3), pl.ds(EX - 3, 3)):
            x0e[:, xs, zs, :] = jnp.zeros((2, 3, HZ, NY), F32)
            a0e[:, xs, zs, :] = jnp.zeros((2, 3, HZ, NY), F32)
        for xs in (pl.ds(0, 4), pl.ds(EX - 4, 4)):
            ce[xs, zs, :] = jnp.zeros((4, HZ, NY), F32)

    lane = iota((1, 128), 1)

    def parts(row, ok):
        value = row * ok
        head = value.astype(BF16).astype(F32)
        return jnp.where(lane < 64, head, value - head)

    def where_points(table, base, dx, dz, width):
        xs = pl.ds(HX, CX) if dx == 0 else land_x(-dx, width)
        zs = pl.ds(HZ, CZ) if dz == 0 else land_z(-dz)
        nx, x_low = (CX, 0) if dx == 0 else ((width, 0) if dx > 0 else (width, CX - width))
        nz, z_low = (CZ, 0) if dz == 0 else ((HZ, 0) if dz > 0 else (HZ, CZ - HZ))
        shape = (nx, nz, 128)
        cell_row = ((iota(shape, 0) + x_low) * CZ + iota(shape, 1) + z_low).reshape(nx * nz, 128).astype(F32)
        hit = cell_row == table[base:base + 1, :]
        along_y = (iota((NY, 128), 0).astype(F32) == table[base + 1:base + 2, :]).astype(F32).astype(BF16)
        return hit, along_y, xs, zs, (nx, nz)

    def place(hit, along_y, rows, shape):
        left = jnp.concatenate([jnp.where(hit, row, 0.0).astype(BF16) for row in rows], axis=0)
        placed = lax.dot_general(left, along_y, (((1,), (1,)), ((), ())), preferred_element_type=F32)
        return placed.reshape((len(rows),) + shape + (NY,))

    def place_sources(table, dx, dz):
        ok = inside(dx, dz)
        hit, along_y, xs, zs, shape = where_points(table, 0, dx, dz, 3)
        srce[:, xs, zs, :] = place(hit, along_y, [parts(table[2 + f:3 + f, :], ok) for f in range(2)], shape)

    def place_own_receivers():
        rows = [own_table[6:7, :]] + [parts(own_table[7 + f:8 + f, :], 1.0) for f in range(2)]
        placed = place(*own_points[:2], rows, own_points[4])
        cnte[...] = placed[0]
        obse[...] = placed[1:3]

    own_table = aux[0:16, :]
    place_sources(own_table, 0, 0)

    loads[8].wait()
    for i, (dx, _) in enumerate(FACES_X):
        for f in range(2):
            ax[i, pl.ds(4 * f, 4)] = a0e[f, send_x(dx, 4), OWN_Z, :].astype(BF16)
    for i, (_, dz) in enumerate(FACES_Z):
        for m, slab in enumerate(pack_face([a0e[f, OWN_X, send_z(dz), :] for f in range(2)], dz)):
            az[i, m] = slab
    for i, (dx, dz) in enumerate(CORNERS):
        tiles = pack_corner(a0e, [layer_at(dx, k, False) for k in (1, 2, 3)], send_z(dz), dz)
        ac[i, 0] = jnp.concatenate(tiles[:2], axis=0).astype(BF16)
        ac[i, 1] = jnp.concatenate([tiles[2], tiles[2]], axis=0).astype(BF16)
    adjoint_halos = []
    for group, s, r in ((FACES_X, ax, bx), (FACES_Z, az, bz), (CORNERS, ac, bc)):
        for i, (dx, dz) in enumerate(group):
            adjoint_halos.append(exchange(len(adjoint_halos), dx, dz, s.at[i], r.at[i], adj_sem))

    lists = pltpu.make_async_remote_copy(
        src_ref=rlist, dst_ref=rlist, send_sem=list_sem.at[0], recv_sem=list_sem.at[1],
        device_id=at(1, 0), device_id_type=MESH)
    lists.wait_recv()
    for n, (dx, dz) in enumerate(AROUND):
        place_sources(rlist[n], -dx, -dz)
    for copy in adjoint_halos:
        copy.start()

    def unpack_face(message, field, zs, ok):
        for m in range(CX // 2):
            slab = message[m].astype(F32) * ok
            for f in range(2):
                tile = slab[8 * f:8 * f + 8]
                field[f, HX + 2 * m, zs, :] = tile
                field[f, HX + 2 * m + 1, zs, :] = pltpu.roll(tile, 4, 0)

    def unpack_corner(message, field, near, zs, ok):
        first, second = message[0].astype(F32) * ok, message[1].astype(F32)
        for f in range(2):
            tile = first[8 * f:8 * f + 8]
            field[f, near[0], zs, :] = tile
            field[f, near[1], zs, :] = pltpu.roll(tile, 4, 0)
        tile = second[0:8] * ok
        field[0, near[2], zs, :] = tile
        field[1, near[2], zs, :] = pltpu.roll(tile, 4, 0)
        return second[8:16]

    for n, (dx, dz) in enumerate(AROUND):
        halos[n].wait_recv()
        ok = inside(-dx, -dz)
        if dz == 0:
            for f in range(2):
                x0e[f, land_x(dx, 4), OWN_Z, :] = rx[n, pl.ds(4 * f, 4)].astype(F32) * ok
            ce[land_x(dx, 3), OWN_Z, :] = rx[n, pl.ds(8, 3)].astype(F32)
        elif dx == 0:
            unpack_face(rz.at[n - 2], x0e, land_z(dz), ok)
            for m in range(2):
                slab = rz[n - 2, 4 + m].astype(F32)
                for k in range(2):
                    tile = slab[8 * k:8 * k + 8]
                    ce[HX + 4 * m + 2 * k, land_z(dz), :] = tile
                    ce[HX + 4 * m + 2 * k + 1, land_z(dz), :] = pltpu.roll(tile, 4, 0)
        else:
            near = [layer_at(dx, k, True) for k in (1, 2, 3)]
            second = unpack_corner(rc.at[n - 4], x0e, near, land_z(dz), ok)
            ce[near[0], land_z(dz), :] = second
            ce[near[1], land_z(dz), :] = pltpu.roll(second, 4, 0)

    lane_row = iota((1, 128), 1)

    def around(ref, f, x):
        c = ref[f, x]
        total = ref[f, x - 1] + ref[f, x + 1]
        total = total + pltpu.roll(c, 1, 0) + pltpu.roll(c, EZ - 1, 0)
        up, down = pltpu.roll(c, 1, 1), pltpu.roll(c, NY - 1, 1)
        low = jnp.where(lane_row == 0, 0.0, up[:, 0:128]) + down[:, 0:128]
        high = up[:, 128:] + jnp.where(lane_row == 127, 0.0, down[:, 128:])
        return c, total + jnp.concatenate([low, high], axis=1)

    def fold(first, second):
        p = first[HZ:HZ + CZ] * second[HZ:HZ + CZ]
        return (p[0:8, 0:128] + p[8:16, 0:128]) + (p[0:8, 128:256] + p[8:16, 128:256])

    def residual_layer(x):
        made = []
        for f in range(2):
            c, total = around(x0e, f, x)
            diag = 6.0 + LAPLACE_SHIFTS[f] * ce[x]
            r = (srce[f, x] - (diag * c - total)) * mask[x]
            v0[f, x] = r
            made.append((r, r))
        return made

    def apply_layer(src, dst):
        def run(x):
            made = []
            for f in range(2):
                c, total = around(src, f, x)
                diag = (6.0 - CENTRE[f]) + LAPLACE_SHIFTS[f] * ce[x]
                new = (diag * c - total) * mask[x]
                if dst is not None:
                    dst[f, x] = new
                made.append((c, new))
            return made
        return run

    def sweep(layer, width, want):
        def outer(t, _):
            layer(HX - 1 - t)
            layer(HX + CX + t)
            return 0

        def summed(t, carry):
            for x in [HX + 8 * t + j for j in range(8)]:
                sums = []
                for c, new in layer(x):
                    for which in want:
                        sums.append(fold(c, new) if which == "cross" else fold(new, new))
                carry = tuple(s + t for s, t in zip(carry, sums))
            return carry

        zero = tuple(jnp.zeros((8, 128), F32) for _ in range(2 * len(want)))
        out = lax.fori_loop(0, CX // 8, summed, zero)
        if width:
            for t in range(width):
                outer(t, 0)
        half = len(want)
        return [(out[i], out[half + i]) for i in range(half)]

    def krylov(widths):
        sums = sweep(apply_layer(v0, v1), widths[0], ("cross", "square"))
        sums += sweep(apply_layer(v1, v2), widths[1], ("cross", "square"))
        sums += sweep(apply_layer(v2, None), 0, ("cross",))
        return sums

    low_lanes = iota((8, 128), 1) < 64
    sub = iota((8, 128), 0)

    def start_sum(stage, value):
        asum[stage] = value
        for i, step in enumerate(PLANE if stage % 2 else COLUMN):
            pltpu.make_async_remote_copy(
                src_ref=asum.at[stage], dst_ref=rsum.at[stage, i],
                send_sem=sum_sem.at[stage, 0], recv_sem=sum_sem.at[stage, 1],
                device_id=beside(step), device_id_type=MESH).start()

    def end_sum(stage):
        everything = pltpu.make_async_remote_copy(
            src_ref=rsum.at[stage], dst_ref=rsum.at[stage],
            send_sem=sum_sem.at[stage, 0], recv_sem=sum_sem.at[stage, 1],
            device_id=at(0, 1), device_id_type=MESH)
        everything.wait_recv()
        return asum[stage] + jnp.sum(rsum[stage], axis=0)

    def pack_sums(sums):
        tile = jnp.zeros((8, 128), F32)
        for k, (s0, s1) in enumerate(sums):
            both = jnp.where(low_lanes, s0 + pltpu.roll(s0, 64, 1), s1 + pltpu.roll(s1, 64, 1))
            tile = jnp.where(sub == k, jnp.sum(both, axis=0, keepdims=True), tile)
        return tile

    def coefficients(tile):
        found = []
        for f in range(2):
            keep = low_lanes if f == 0 else jnp.logical_not(low_lanes)
            column = jnp.sum(jnp.where(keep, tile, 0.0), axis=1, keepdims=True)
            nu = [column[k:k + 1, :] for k in range(2 * ITERS)]
            found.append(cg_coefficients(nu, CENTRE[f]))
        return found

    sums = sweep(residual_layer, 3, ("square",))
    sums += krylov((2, 1))
    start_sum(0, pack_sums(sums))

    for i, step in enumerate(LAYERS):
        pltpu.make_async_remote_copy(
            src_ref=aux.at[pl.ds(16, 16)], dst_ref=cols.at[i], send_sem=cols_sem.at[0], recv_sem=cols_sem.at[1],
            device_id=beside(step), device_id_type=MESH).start()

    own_points = where_points(own_table, 4, 0, 0, 0)
    place_own_receivers()
    here = jnp.where(own_points[0], 1.0, 0.0)
    fields = []
    for ref in (x0e, v0, v1, v2):
        for f in range(2):
            fields.append(ref[f, OWN_X, OWN_Z, :].reshape(ROWS, NY))
    fields = jnp.concatenate(fields, axis=0)
    head = fields.astype(BF16)
    tail = (fields - head.astype(F32)).astype(BF16)
    columns = lax.dot_general(head, own_points[1], (((1,), (0,)), ((), ())), preferred_element_type=F32)
    columns += lax.dot_general(tail, own_points[1], (((1,), (0,)), ((), ())), preferred_element_type=F32)
    for j in range(8):
        row = jnp.sum(columns[ROWS * j:ROWS * (j + 1)] * here, axis=0, keepdims=True)
        seen[j:j + 1, :] = row - own_table[7 + j:8 + j, :] if j < 2 else row
    for n, (dx, dz) in enumerate(AROUND):
        pltpu.make_async_remote_copy(
            src_ref=seen, dst_ref=rseen.at[n], send_sem=seen_sem.at[0], recv_sem=seen_sem.at[1],
            device_id=at(dx, dz), device_id_type=MESH).start()
    point_values = pltpu.make_async_remote_copy(
        src_ref=rseen, dst_ref=rseen, send_sem=seen_sem.at[0], recv_sem=seen_sem.at[1],
        device_id=at(1, 0), device_id_type=MESH)
    around_points = []
    for n, (dx, dz) in enumerate(AROUND):
        hit, along_y, xs, zs, shape = where_points(rlist[n], 4, -dx, -dz, 3)
        rec_y[n] = along_y
        count = shape[0] * shape[1]
        rec_hit[n, pl.ds(0, count)] = jnp.where(hit, 1.0, 0.0)
        around_points.append((xs, zs, shape, count))
    for n, (dx, dz) in enumerate(AROUND):
        adjoint_halos[n].wait_recv()
        ok = inside(-dx, -dz)
        if dz == 0:
            for f in range(2):
                a0e[f, land_x(dx, 4), OWN_Z, :] = bx[n, pl.ds(4 * f, 4)].astype(F32) * ok
        elif dx == 0:
            unpack_face(bz.at[n - 2], a0e, land_z(dz), ok)
        else:
            unpack_corner(bc.at[n - 4], a0e, [layer_at(dx, k, True) for k in (1, 2, 3)], land_z(dz), ok)

    start_sum(1, end_sum(0))

    def adjoint_part(t, _):
        for x in (HX - 3 + 2 * t, HX - 2 + 2 * t):
            for f in range(2):
                c, total = around(a0e, f, x)
                diag = 6.0 + LAPLACE_SHIFTS[f] * ce[x]
                w[f, x] = (diag * c - total) * mask[x]
        return 0

    for t in range(CX // 2 + 3):
        adjoint_part(t, 0)

    pltpu.make_async_remote_copy(
        src_ref=cols.at[pl.ds(0, NB - 1)], dst_ref=cols.at[pl.ds(0, NB - 1)],
        send_sem=cols_sem.at[0], recv_sem=cols_sem.at[1],
        device_id=at(0, 1), device_id_type=MESH).wait_recv()
    cols[NB - 1] = aux[16:32, :]
    first_row = (d * ROWS).astype(F32)
    row_lane = iota((NNZ, 128), 1).astype(F32)

    def request(slot, _):
        row = 2.0 * cols[slot] - first_row
        hot = jnp.concatenate([jnp.where(row == row_lane, 1.0, 0.0), jnp.where(row + 1.0 == row_lane, 1.0, 0.0)], axis=0)
        pick_hot[pl.ds(slot * 2 * NNZ, 2 * NNZ)] = hot.astype(BF16)
        return 0

    for slot in range(NB):
        request(slot, 0)

    point_values.wait_recv()
    found = coefficients(end_sum(1))

    for n, (dx, dz) in enumerate(AROUND):
        xs, zs, shape, count = around_points[n]
        ok = inside(-dx, -dz)
        left = []
        for f in range(2):
            a = found[f]
            values = rseen[n, f:f + 1, :]
            for k in range(ITERS):
                values = values + a[k] * rseen[n, 2 * (k + 1) + f:2 * (k + 1) + f + 1, :]
            left.append((rec_hit[n, pl.ds(0, count)] * parts(values, ok)).astype(BF16))
        placed = lax.dot_general(jnp.concatenate(left, axis=0), rec_y[n], (((1,), (1,)), ((), ())),
                                 preferred_element_type=F32).reshape((2,) + shape + (NY,))
        v0[:, xs, zs, :] = placed - w[:, xs, zs, :]

    def own_residual(t, carry):
        for x in [HX + 8 * t + j for j in range(8)]:
            out = []
            for f in range(2):
                a = found[f]
                new = x0e[f, x, OWN_Z, :] + a[0] * v0[f, x, OWN_Z, :] + a[1] * v1[f, x, OWN_Z, :]
                new = new + a[2] * v2[f, x, OWN_Z, :]
                fwd[f, x - HX] = new
                u = cnte[x - HX] * new - obse[f, x - HX] - w[f, x, OWN_Z, :]
                v0[f, x, OWN_Z, :] = u
                p = u * u
                out.append(carry[f] + (p[0:8, 0:128] + p[8:16, 0:128]) + (p[0:8, 128:256] + p[8:16, 128:256]))
            carry = tuple(out)
        return carry

    squares = lax.fori_loop(0, CX // 8, own_residual, (jnp.zeros((8, 128), F32),) * 2)
    forward_store = pltpu.make_async_copy(fwd, fwd_out, out_sem.at[0])
    forward_store.start()

    sums = [squares] + krylov((2, 1))
    start_sum(2, pack_sums(sums))
    start_sum(3, end_sum(2))
    found_adjoint = coefficients(end_sum(3))

    def gradient_layer(x, _):
        total = jnp.zeros((CZ, NY), F32)
        for f in range(2):
            e = found_adjoint[f]
            own = a0e[f, x + HX, OWN_Z, :] + e[0] * v0[f, x + HX, OWN_Z, :] + e[1] * v1[f, x + HX, OWN_Z, :]
            own = own + e[2] * v2[f, x + HX, OWN_Z, :]
            total = total + LAPLACE_SHIFTS[f] * fwd[f, x] * own
        grad[pl.ds(x * CZ, CZ)] = (-total).astype(BF16)
        return 0

    for x in range(CX):
        gradient_layer(x, 0)

    psend[...] = jnp.dot(pick_hot[...], grad[...], preferred_element_type=F32).astype(BF16).reshape(NB, 2 * NNZ, NY)

    for i, step in enumerate(LAYERS):
        back = ((4 - step[0]) % 4,) + step[1:]
        pltpu.make_async_remote_copy(
            src_ref=psend.at[i], dst_ref=precv.at[i], send_sem=pick_sem.at[0], recv_sem=pick_sem.at[1],
            device_id=beside(back), device_id_type=MESH).start()

    cov_load.wait()
    picks = pltpu.make_async_remote_copy(
        src_ref=precv, dst_ref=precv, send_sem=pick_sem.at[0], recv_sem=pick_sem.at[1],
        device_id=at(0, 1), device_id_type=MESH)
    picks.wait_recv()
    picked = psend[NB - 1].astype(F32) + jnp.sum(precv[...].astype(F32), axis=0)
    picked = picked.astype(BF16)

    term_row = iota((NNZ, BLOCK), 0)

    def term(t, total):
        for k in range(NNZ):
            block = cov[k]
            made = lax.dot_general(picked[0:NNZ], block[:, 0:NY], (((1,), (1,)), ((), ())), preferred_element_type=F32)
            made += lax.dot_general(picked[NNZ:], block[:, NY:], (((1,), (1,)), ((), ())), preferred_element_type=F32)
            total = jnp.where(term_row == k, made, total)
        return total

    terms = lax.fori_loop(0, 1, term, jnp.zeros((NNZ, BLOCK), F32))
    cov_rows = rows_v[0].astype(F32)
    out_row = iota((ROWS, NNZ), 0).astype(F32)
    total = grad[...].astype(F32)
    for half in range(2):
        hot = jnp.where(2.0 * cov_rows + float(half) == out_row, 1.0, 0.0)
        total = total + jnp.dot(hot, terms[:, half * NY:(half + 1) * NY], precision=lax.Precision.HIGHEST,
                                preferred_element_type=F32)
    pre[...] = total.reshape(CX, CZ, NY)
    pre_store = pltpu.make_async_copy(pre, pre_out, out_sem.at[1])
    pre_store.start()

    lists.wait_send()
    for copy in halos + adjoint_halos + [point_values]:
        copy.wait_send()
    pltpu.make_async_remote_copy(
        src_ref=cols.at[pl.ds(0, NB - 1)], dst_ref=cols.at[pl.ds(0, NB - 1)],
        send_sem=cols_sem.at[0], recv_sem=cols_sem.at[1],
        device_id=at(0, 1), device_id_type=MESH).wait_send()
    for stage in range(4):
        pltpu.make_async_remote_copy(
            src_ref=rsum.at[stage], dst_ref=rsum.at[stage],
            send_sem=sum_sem.at[stage, 0], recv_sem=sum_sem.at[stage, 1],
            device_id=at(0, 1), device_id_type=MESH).wait_send()
    picks.wait_send()
    forward_store.wait()
    pre_store.wait()


def hand_over(fwd_in, pre_in, fwd_out, pre_out):
    fwd_out[...] = fwd_in[...]
    pre_out[...] = pre_in[...]


def local(conductivity, initial_field, adjoint_initial, src_cell, src_amp, rec_cell, observed, cov_blocks, cov_rows, cov_cols):
    big = pltpu.VMEM((2, EX, EZ, NY), F32)
    one = pltpu.VMEM((EX, EZ, NY), F32)
    dma = pltpu.SemaphoreType.DMA
    scratch = [
        pltpu.VMEM(src_cell.shape, jnp.int32), pltpu.VMEM(src_amp.shape, F32),
        pltpu.VMEM(rec_cell.shape, jnp.int32), pltpu.VMEM(observed.shape, F32),
        pltpu.VMEM(cov_rows.shape, jnp.int32), pltpu.VMEM(cov_cols.shape, jnp.int32),
        pltpu.VMEM((32, 128), F32), pltpu.VMEM((NNZ, BLOCK, BLOCK), BF16),
        one, big, big, one, big,
        pltpu.VMEM((2, CX, CZ, NY), F32), pltpu.VMEM((CX, CZ, NY), F32),
        big, big, big, big,
        pltpu.VMEM((2, CX, CZ, NY), F32), pltpu.VMEM((ROWS, NY), BF16), pltpu.VMEM((CX, CZ, NY), F32),
        pltpu.VMEM((2 * NNZ * NB, ROWS), BF16),
    ]
    for count, slabs in ((2, 11), (2, 6), (4, 2), (2, 8), (2, 4), (4, 2)):
        scratch += [pltpu.VMEM((count, slabs, 16, NY), BF16)] * 2
    scratch += [
        pltpu.VMEM((8, 16, 128), F32), pltpu.VMEM((8, 128), F32), pltpu.VMEM((8, 8, 128), F32),
        pltpu.VMEM((8, 64, 128), F32), pltpu.VMEM((8, NY, 128), BF16), pltpu.VMEM((NB, NNZ, 128), F32),
        pltpu.VMEM((4, 8, 128), F32), pltpu.VMEM((4, NB - 1, 8, 128), F32),
        pltpu.VMEM((NB, 2 * NNZ, NY), BF16), pltpu.VMEM((NB - 1, 2 * NNZ, NY), BF16),
        dma((9,)), dma, dma((2,)), dma((2,)), dma((2,)), dma((8, 2)), dma((8, 2)), dma((2,)), dma((4, 2)), dma((2,)),
    ]
    anywhere = pl.BlockSpec(memory_space=pl.ANY)
    results = pl.pallas_call(
        kernel,
        out_shape=(
            jax.ShapeDtypeStruct((2, CX, CZ, NY), F32),
            jax.ShapeDtypeStruct((CX, CZ, NY), F32),
        ),
        in_specs=[anywhere] * 10,
        out_specs=(anywhere, anywhere),
        scratch_shapes=scratch,
        compiler_params=pltpu.CompilerParams(
            collective_id=0, has_side_effects=True, vmem_limit_bytes=56 * 2**20),
    )(conductivity, initial_field, adjoint_initial, src_cell, src_amp, rec_cell, observed,
      cov_blocks.reshape(NNZ, BLOCK, BLOCK), cov_rows, cov_cols)
    return pl.pallas_call(
        hand_over,
        out_shape=[jax.ShapeDtypeStruct(r.shape, r.dtype) for r in results],
    )(*results)


def solution(mesh):
    return jax.shard_map(
        local,
        mesh=mesh,
        in_specs=(
            P("brick", "depth", None),
            P(None, "brick", "depth", None),
            P(None, "brick", "depth", None),
            P("brick", "depth", None),
            P("brick", "depth", None, None),
            P("brick", "depth", None),
            P("brick", "depth", None, None),
            P("brick", "depth", None, None, None),
            P("brick", "depth", None),
            P("brick", "depth", None),
        ),
        out_specs=(P(None, "brick", "depth", None), P("brick", "depth", None)),
        check_vma=False,
    )
```

```python
import functools

import jax
import jax.numpy as jnp
from jax import lax
from jax.experimental import pallas as pl
from jax.experimental.pallas import tpu as pltpu
from jax.sharding import PartitionSpec as P

LAPLACE_SHIFTS = (0.5, 2.0)
CENTRE = (6.5, 8.0)
ITERS = 3
NB = 16
CX, CZ, NY = 8, 16, 256
HX, HZ = 6, 8
EX, EZ = CX + 2 * HX, CZ + 2 * HZ
NNZ, BLOCK = 16, 512
ROWS = CX * CZ
F32, BF16 = jnp.float32, jnp.bfloat16
MESH = pl.DeviceIdType.MESH
OWN_X, OWN_Z = pl.ds(HX, CX), pl.ds(HZ, CZ)

FACES_X = ((1, 0), (-1, 0))
FACES_Z = ((0, 1), (0, -1))
CORNERS = ((1, 1), (1, -1), (-1, 1), (-1, -1))
AROUND = FACES_X + FACES_Z + CORNERS

STEPS = sorted(
    ((i, j, k, c) for i in range(4) for j in range(4) for k in range(8) for c in range(2)),
    key=lambda s: -(8 * (min(s[0], 4 - s[0]) + min(s[1], 4 - s[1]) + min(s[2], 8 - s[2])) + s[3]))
PLANE = [s for s in STEPS if s[2:] == (0, 0) and s[:2] != (0, 0)]
COLUMN = [s for s in STEPS if s[:2] == (0, 0) and s[2:] != (0, 0)]
LAYERS = [s for s in STEPS if s[2] == 0 and s[1] % 2 == 0 and s != (0, 0, 0, 0)]


def iota(shape, dim):
    return lax.broadcasted_iota(jnp.int32, shape, dim)


def send_x(dx, width, skip=0):
    return pl.ds(HX + CX - skip - width, width) if dx > 0 else pl.ds(HX + skip, width)


def send_z(dz):
    return pl.ds(HZ + CZ - HZ, HZ) if dz > 0 else pl.ds(HZ, HZ)


def land_x(dx, width, skip=0):
    return pl.ds(HX - skip - width, width) if dx > 0 else pl.ds(HX + CX + skip, width)


def land_z(dz):
    return pl.ds(0, HZ) if dz > 0 else pl.ds(HZ + CZ, HZ)


def layer_at(dx, distance, land):
    if land:
        return HX - distance if dx > 0 else HX + CX + distance - 1
    return HX + CX - distance if dx > 0 else HX + distance - 1


def halves(first, second, dz):
    near = (iota((8, 1), 0) >= 4) if dz > 0 else (iota((8, 1), 0) < 4)
    return jnp.where(near, first, pltpu.roll(second, 4, 0))


def pack_face(field, dz):
    slabs = []
    for m in range(CX // 2):
        tiles = [halves(field[f][2 * m], field[f][2 * m + 1], dz) for f in range(2)]
        slabs.append(jnp.concatenate(tiles, axis=0).astype(BF16))
    return slabs


def pack_corner(field, near, zs, dz):
    tiles = [halves(field[f, near[0], zs, :], field[f, near[1], zs, :], dz) for f in range(2)]
    return tiles + [halves(field[0, near[2], zs, :], field[1, near[2], zs, :], dz)]


def cg_coefficients(nu, centre):
    def inner(p, q, shift):
        total = None
        for i, pi in enumerate(p):
            for j, qj in enumerate(q):
                term = pi * qj * nu[i + j + shift]
                total = term if total is None else total + term
        return total

    one = jnp.ones_like(nu[0])
    r, p = [one], [one]
    rr = nu[0]
    x = [jnp.zeros_like(one)] * ITERS
    for it in range(ITERS):
        step = rr / (inner(p, p, 1) + centre * inner(p, p, 0))
        for i, pi in enumerate(p):
            x[i] = x[i] + step * pi
        if it + 1 < ITERS:
            ap = [centre * pi for pi in p] + [jnp.zeros_like(one)]
            for i, pi in enumerate(p):
                ap[i + 1] = ap[i + 1] + pi
            r = r + [jnp.zeros_like(one)]
            r = [ri - step * ai for ri, ai in zip(r, ap)]
            new = inner(r, r, 0)
            beta = new / rr
            p = p + [jnp.zeros_like(one)]
            p = [ri + beta * pi for ri, pi in zip(r, p)]
            rr = new
    return x


def kernel(
    cond_in, x0_in, a0_in, src_in, amp_in, rec_in, obs_in, cov_in, rows_in, cols_in,
    fwd_out, pre_out,
    src_v, amp_v, rec_v, obs_v, rows_v, cols_v, aux, cov, ce, x0e, a0e, mask, srce, obse, cnte, v0, v1, v2, w, diagonal, fwd, grad, pre, pick_hot,
    sx, rx, sz, rz, sc, rc, ax, bx, az, bz, ac, bc,
    rlist, seen, rseen, rec_hit, rec_y, cols, asum, rsum, psend, precv,
    in_sem, cov_sem, out_sem, list_sem, cols_sem, halo_sem, adj_sem, seen_sem, sum_sem, pick_sem,
):
    b, d = lax.axis_index("brick"), lax.axis_index("depth")

    def at(dx, dz):
        return lax.rem(b + dx + NB, NB), lax.rem(d + dz + NB, NB)

    barrier = pltpu.get_barrier_semaphore()
    for dx, dz in FACES_X + CORNERS:
        pl.semaphore_signal(barrier, inc=1, device_id=at(dx, dz), device_id_type=MESH)

    cx, cy = lax.div(d, 4), 2 * lax.rem(lax.div(d, 2), 2) + lax.div(b, 8)
    cz, core = lax.rem(b, 8), lax.rem(d, 2)

    def beside(step):
        x, y = lax.rem(cx + step[0], 4), lax.rem(cy + step[1], 4)
        return lax.rem(y, 2) * 8 + lax.rem(cz + step[2], 8), x * 4 + lax.div(y, 2) * 2 + lax.rem(core + step[3], 2)

    greeted = LAYERS + [s for s in PLANE if s[1] % 2] + [s for s in COLUMN if s[2]]
    for step in greeted:
        pl.semaphore_signal(barrier, inc=1, device_id=beside(step), device_id_type=MESH)

    loads = [
        pltpu.make_async_copy(x0_in, x0e.at[:, OWN_X, OWN_Z, :], in_sem.at[0]),
        pltpu.make_async_copy(cond_in, ce.at[OWN_X, OWN_Z, :], in_sem.at[1]),
        pltpu.make_async_copy(src_in, src_v, in_sem.at[2]),
        pltpu.make_async_copy(amp_in, amp_v, in_sem.at[3]),
        pltpu.make_async_copy(rec_in, rec_v, in_sem.at[4]),
        pltpu.make_async_copy(obs_in, obs_v, in_sem.at[5]),
        pltpu.make_async_copy(rows_in, rows_v, in_sem.at[6]),
        pltpu.make_async_copy(cols_in, cols_v, in_sem.at[7]),
        pltpu.make_async_copy(a0_in, a0e.at[:, OWN_X, OWN_Z, :], in_sem.at[8]),
    ]
    for load in loads:
        load.start()
    cov_load = pltpu.make_async_copy(cov_in, cov, cov_sem)
    cov_load.start()

    for load in loads[:2]:
        load.wait()
    for i, (dx, _) in enumerate(FACES_X):
        for f in range(2):
            sx[i, pl.ds(4 * f, 4)] = x0e[f, send_x(dx, 4), OWN_Z, :].astype(BF16)
        sx[i, pl.ds(8, 3)] = ce[send_x(dx, 3), OWN_Z, :].astype(BF16)
    for i, (_, dz) in enumerate(FACES_Z):
        zs = send_z(dz)
        for m, slab in enumerate(pack_face([x0e[f, OWN_X, zs, :] for f in range(2)], dz)):
            sz[i, m] = slab
        for m in range(2):
            tiles = [halves(ce[HX + k, zs, :], ce[HX + k + 1, zs, :], dz) for k in (4 * m, 4 * m + 2)]
            sz[i, 4 + m] = jnp.concatenate(tiles, axis=0).astype(BF16)
    for i, (dx, dz) in enumerate(CORNERS):
        zs = send_z(dz)
        near = [layer_at(dx, k, False) for k in (1, 2, 3)]
        tiles = pack_corner(x0e, near, zs, dz)
        tiles.append(halves(ce[near[0], zs, :], ce[near[1], zs, :], dz))
        sc[i, 0] = jnp.concatenate(tiles[:2], axis=0).astype(BF16)
        sc[i, 1] = jnp.concatenate(tiles[2:], axis=0).astype(BF16)

    for load in loads[2:8]:
        load.wait()

    def twice(row):
        return jnp.concatenate([row, row], axis=1)

    src_cell, rec_cell = src_v[0], rec_v[0]
    aux[0:1, :] = twice((src_cell >> 8).astype(F32))
    aux[1:2, :] = twice((src_cell & (NY - 1)).astype(F32))
    aux[2:4, :] = twice(amp_v[0, 0])
    aux[4:5, :] = twice((rec_cell >> 8).astype(F32))
    aux[5:6, :] = twice((rec_cell & (NY - 1)).astype(F32))
    aux[6:7, :] = jnp.where(iota((1, 128), 1) < 64, 1.0, 0.0)
    aux[7:9, :] = twice(obs_v[0, 0])
    aux[9:16, :] = jnp.zeros((7, 128), F32)
    col_row = jnp.where(iota((NNZ, NNZ), 0) == iota((NNZ, NNZ), 1), cols_v[0].astype(F32), 0.0)
    aux[16:32, :] = jnp.broadcast_to(jnp.sum(col_row, axis=1, keepdims=True), (NNZ, 128))

    pl.semaphore_wait(barrier, len(FACES_X) + len(CORNERS) + len(greeted))

    for n, (dx, dz) in enumerate(AROUND):
        pltpu.make_async_remote_copy(
            src_ref=aux.at[pl.ds(0, 16)], dst_ref=rlist.at[n], send_sem=list_sem.at[0], recv_sem=list_sem.at[1],
            device_id=at(dx, dz), device_id_type=MESH).start()

    def exchange(n, dx, dz, src, dst, sems):
        return pltpu.make_async_remote_copy(
            src_ref=src, dst_ref=dst, send_sem=sems.at[n, 0], recv_sem=sems.at[n, 1],
            device_id=at(dx, dz), device_id_type=MESH)

    halos = []
    for group, s, r in ((FACES_X, sx, rx), (FACES_Z, sz, rz), (CORNERS, sc, rc)):
        for i, (dx, dz) in enumerate(group):
            halos.append(exchange(len(halos), dx, dz, s.at[i], r.at[i], halo_sem))
    for copy in reversed(halos):
        copy.start()

    def inside(dx, dz):
        bx_, dz_ = b + dx, d + dz
        ok = (bx_ >= 0) & (bx_ < NB) & (dz_ >= 0) & (dz_ < NB)
        return jnp.where(ok, 1.0, 0.0).astype(F32)

    for i, (dx, dz) in enumerate(((0, 0),) + AROUND):
        xs = pl.ds(HX, CX) if dx == 0 else land_x(-dx, HX)
        zs = pl.ds(HZ, CZ) if dz == 0 else land_z(-dz)
        nx, nz = (CX if dx == 0 else HX), (CZ if dz == 0 else HZ)
        mask[xs, zs, :] = jnp.full((nx, nz, NY), inside(dx, dz), F32)

    for zs in (pl.ds(0, HZ), pl.ds(HZ + CZ, HZ)):
        for xs in (pl.ds(0, 3), pl.ds(EX - 3, 3)):
            x0e[:, xs, zs, :] = jnp.zeros((2, 3, HZ, NY), F32)
            a0e[:, xs, zs, :] = jnp.zeros((2, 3, HZ, NY), F32)
        for xs in (pl.ds(0, 4), pl.ds(EX - 4, 4)):
            ce[xs, zs, :] = jnp.zeros((4, HZ, NY), F32)

    lane = iota((1, 128), 1)

    def parts(row, ok):
        value = row * ok
        head = value.astype(BF16).astype(F32)
        return jnp.where(lane < 64, head, value - head)

    def where_points(table, base, dx, dz, width):
        xs = pl.ds(HX, CX) if dx == 0 else land_x(-dx, width)
        zs = pl.ds(HZ, CZ) if dz == 0 else land_z(-dz)
        nx, x_low = (CX, 0) if dx == 0 else ((width, 0) if dx > 0 else (width, CX - width))
        nz, z_low = (CZ, 0) if dz == 0 else ((HZ, 0) if dz > 0 else (HZ, CZ - HZ))
        shape = (nx, nz, 128)
        cell_row = ((iota(shape, 0) + x_low) * CZ + iota(shape, 1) + z_low).reshape(nx * nz, 128).astype(F32)
        hit = cell_row == table[base:base + 1, :]
        along_y = (iota((NY, 128), 0).astype(F32) == table[base + 1:base + 2, :]).astype(F32).astype(BF16)
        return hit, along_y, xs, zs, (nx, nz)

    def place(hit, along_y, rows, shape):
        left = jnp.concatenate([jnp.where(hit, row, 0.0).astype(BF16) for row in rows], axis=0)
        placed = lax.dot_general(left, along_y, (((1,), (1,)), ((), ())), preferred_element_type=F32)
        return placed.reshape((len(rows),) + shape + (NY,))

    def place_sources(table, dx, dz):
        ok = inside(dx, dz)
        hit, along_y, xs, zs, shape = where_points(table, 0, dx, dz, 3)
        srce[:, xs, zs, :] = place(hit, along_y, [parts(table[2 + f:3 + f, :], ok) for f in range(2)], shape)

    def place_own_receivers():
        rows = [own_table[6:7, :]] + [parts(own_table[7 + f:8 + f, :], 1.0) for f in range(2)]
        placed = place(*own_points[:2], rows, own_points[4])
        cnte[...] = placed[0]
        obse[...] = placed[1:3]

    own_table = aux[0:16, :]
    place_sources(own_table, 0, 0)

    loads[8].wait()
    for i, (dx, _) in enumerate(FACES_X):
        for f in range(2):
            ax[i, pl.ds(4 * f, 4)] = a0e[f, send_x(dx, 4), OWN_Z, :].astype(BF16)
    for i, (_, dz) in enumerate(FACES_Z):
        for m, slab in enumerate(pack_face([a0e[f, OWN_X, send_z(dz), :] for f in range(2)], dz)):
            az[i, m] = slab
    for i, (dx, dz) in enumerate(CORNERS):
        tiles = pack_corner(a0e, [layer_at(dx, k, False) for k in (1, 2, 3)], send_z(dz), dz)
        ac[i, 0] = jnp.concatenate(tiles[:2], axis=0).astype(BF16)
        ac[i, 1] = jnp.concatenate([tiles[2], tiles[2]], axis=0).astype(BF16)
    adjoint_halos = []
    for group, s, r in ((FACES_X, ax, bx), (FACES_Z, az, bz), (CORNERS, ac, bc)):
        for i, (dx, dz) in enumerate(group):
            adjoint_halos.append(exchange(len(adjoint_halos), dx, dz, s.at[i], r.at[i], adj_sem))

    lists = pltpu.make_async_remote_copy(
        src_ref=rlist, dst_ref=rlist, send_sem=list_sem.at[0], recv_sem=list_sem.at[1],
        device_id=at(1, 0), device_id_type=MESH)
    lists.wait_recv()
    for n, (dx, dz) in enumerate(AROUND):
        place_sources(rlist[n], -dx, -dz)
    for copy in adjoint_halos:
        copy.start()

    def unpack_face(message, field, zs, ok):
        for m in range(CX // 2):
            slab = message[m].astype(F32) * ok
            for f in range(2):
                tile = slab[8 * f:8 * f + 8]
                field[f, HX + 2 * m, zs, :] = tile
                field[f, HX + 2 * m + 1, zs, :] = pltpu.roll(tile, 4, 0)

    def unpack_corner(message, field, near, zs, ok):
        first, second = message[0].astype(F32) * ok, message[1].astype(F32)
        for f in range(2):
            tile = first[8 * f:8 * f + 8]
            field[f, near[0], zs, :] = tile
            field[f, near[1], zs, :] = pltpu.roll(tile, 4, 0)
        tile = second[0:8] * ok
        field[0, near[2], zs, :] = tile
        field[1, near[2], zs, :] = pltpu.roll(tile, 4, 0)
        return second[8:16]

    for n, (dx, dz) in enumerate(AROUND):
        halos[n].wait_recv()
        ok = inside(-dx, -dz)
        if dz == 0:
            for f in range(2):
                x0e[f, land_x(dx, 4), OWN_Z, :] = rx[n, pl.ds(4 * f, 4)].astype(F32) * ok
            ce[land_x(dx, 3), OWN_Z, :] = rx[n, pl.ds(8, 3)].astype(F32)
        elif dx == 0:
            unpack_face(rz.at[n - 2], x0e, land_z(dz), ok)
            for m in range(2):
                slab = rz[n - 2, 4 + m].astype(F32)
                for k in range(2):
                    tile = slab[8 * k:8 * k + 8]
                    ce[HX + 4 * m + 2 * k, land_z(dz), :] = tile
                    ce[HX + 4 * m + 2 * k + 1, land_z(dz), :] = pltpu.roll(tile, 4, 0)
        else:
            near = [layer_at(dx, k, True) for k in (1, 2, 3)]
            second = unpack_corner(rc.at[n - 4], x0e, near, land_z(dz), ok)
            ce[near[0], land_z(dz), :] = second
            ce[near[1], land_z(dz), :] = pltpu.roll(second, 4, 0)

    lane_row = iota((1, 128), 1)

    def around(ref, f, x):
        c = ref[f, x]
        total = ref[f, x - 1] + ref[f, x + 1]
        total = total + pltpu.roll(c, 1, 0) + pltpu.roll(c, EZ - 1, 0)
        up, down = pltpu.roll(c, 1, 1), pltpu.roll(c, NY - 1, 1)
        low = jnp.where(lane_row == 0, 0.0, up[:, 0:128]) + down[:, 0:128]
        high = up[:, 128:] + jnp.where(lane_row == 127, 0.0, down[:, 128:])
        return c, total + jnp.concatenate([low, high], axis=1)

    def fold(first, second):
        p = first[HZ:HZ + CZ] * second[HZ:HZ + CZ]
        return (p[0:8, 0:128] + p[8:16, 0:128]) + (p[0:8, 128:256] + p[8:16, 128:256])

    def residual_layer(x):
        made = []
        for f in range(2):
            c, total = around(x0e, f, x)
            diag = 6.0 + LAPLACE_SHIFTS[f] * ce[x]
            r = (srce[f, x] - (diag * c - total)) * mask[x]
            v0[f, x] = r
            made.append((r, r))
        return made

    def apply_layer(src, dst, ready=False):
        def run(x):
            made = []
            for f in range(2):
                c, total = around(src, f, x)
                if ready:
                    new = diagonal[f, x] * c - total * mask[x]
                else:
                    diag = (6.0 - CENTRE[f]) + LAPLACE_SHIFTS[f] * ce[x]
                    new = (diag * c - total) * mask[x]
                if dst is not None:
                    dst[f, x] = new
                made.append((c, new))
            return made
        return run

    def sweep(layer, width, want):
        def outer(t, _):
            layer(HX - 1 - t)
            layer(HX + CX + t)
            return 0

        def summed(t, carry):
            for x in [HX + 8 * t + j for j in range(8)]:
                sums = []
                for c, new in layer(x):
                    for which in want:
                        sums.append(fold(c, new) if which == "cross" else fold(new, new))
                carry = tuple(s + t for s, t in zip(carry, sums))
            return carry

        zero = tuple(jnp.zeros((8, 128), F32) for _ in range(2 * len(want)))
        out = lax.fori_loop(0, CX // 8, summed, zero)
        if width:
            for t in range(width):
                outer(t, 0)
        half = len(want)
        return [(out[i], out[half + i]) for i in range(half)]

    def krylov(widths, ready=False):
        sums = sweep(apply_layer(v0, v1, ready), widths[0], ("cross", "square"))
        sums += sweep(apply_layer(v1, v2, ready), widths[1], ("cross", "square"))
        sums += sweep(apply_layer(v2, None, ready), 0, ("cross",))
        return sums

    low_lanes = iota((8, 128), 1) < 64
    sub = iota((8, 128), 0)

    def start_sum(stage, value):
        asum[stage] = value
        for i, step in enumerate(PLANE if stage % 2 else COLUMN):
            pltpu.make_async_remote_copy(
                src_ref=asum.at[stage], dst_ref=rsum.at[stage, i],
                send_sem=sum_sem.at[stage, 0], recv_sem=sum_sem.at[stage, 1],
                device_id=beside(step), device_id_type=MESH).start()

    def end_sum(stage):
        everything = pltpu.make_async_remote_copy(
            src_ref=rsum.at[stage], dst_ref=rsum.at[stage],
            send_sem=sum_sem.at[stage, 0], recv_sem=sum_sem.at[stage, 1],
            device_id=at(0, 1), device_id_type=MESH)
        everything.wait_recv()
        return asum[stage] + jnp.sum(rsum[stage], axis=0)

    def pack_sums(sums):
        tile = jnp.zeros((8, 128), F32)
        for k, (s0, s1) in enumerate(sums):
            both = jnp.where(low_lanes, s0 + pltpu.roll(s0, 64, 1), s1 + pltpu.roll(s1, 64, 1))
            tile = jnp.where(sub == k, jnp.sum(both, axis=0, keepdims=True), tile)
        return tile

    def coefficients(tile):
        found = []
        for f in range(2):
            keep = low_lanes if f == 0 else jnp.logical_not(low_lanes)
            column = jnp.sum(jnp.where(keep, tile, 0.0), axis=1, keepdims=True)
            nu = [column[k:k + 1, :] for k in range(2 * ITERS)]
            found.append(cg_coefficients(nu, CENTRE[f]))
        return found

    sums = sweep(residual_layer, 3, ("square",))
    sums += krylov((2, 1))
    start_sum(0, pack_sums(sums))

    for i, step in enumerate(LAYERS):
        pltpu.make_async_remote_copy(
            src_ref=aux.at[pl.ds(16, 16)], dst_ref=cols.at[i], send_sem=cols_sem.at[0], recv_sem=cols_sem.at[1],
            device_id=beside(step), device_id_type=MESH).start()

    own_points = where_points(own_table, 4, 0, 0, 0)
    place_own_receivers()
    here = jnp.where(own_points[0], 1.0, 0.0)
    fields = []
    for ref in (x0e, v0, v1, v2):
        for f in range(2):
            fields.append(ref[f, OWN_X, OWN_Z, :].reshape(ROWS, NY))
    fields = jnp.concatenate(fields, axis=0)
    head = fields.astype(BF16)
    tail = (fields - head.astype(F32)).astype(BF16)
    columns = lax.dot_general(head, own_points[1], (((1,), (0,)), ((), ())), preferred_element_type=F32)
    columns += lax.dot_general(tail, own_points[1], (((1,), (0,)), ((), ())), preferred_element_type=F32)
    for j in range(8):
        row = jnp.sum(columns[ROWS * j:ROWS * (j + 1)] * here, axis=0, keepdims=True)
        seen[j:j + 1, :] = row - own_table[7 + j:8 + j, :] if j < 2 else row
    for n, (dx, dz) in enumerate(AROUND):
        pltpu.make_async_remote_copy(
            src_ref=seen, dst_ref=rseen.at[n], send_sem=seen_sem.at[0], recv_sem=seen_sem.at[1],
            device_id=at(dx, dz), device_id_type=MESH).start()
    point_values = pltpu.make_async_remote_copy(
        src_ref=rseen, dst_ref=rseen, send_sem=seen_sem.at[0], recv_sem=seen_sem.at[1],
        device_id=at(1, 0), device_id_type=MESH)
    around_points = []
    for n, (dx, dz) in enumerate(AROUND):
        hit, along_y, xs, zs, shape = where_points(rlist[n], 4, -dx, -dz, 3)
        rec_y[n] = along_y
        count = shape[0] * shape[1]
        rec_hit[n, pl.ds(0, count)] = jnp.where(hit, 1.0, 0.0)
        around_points.append((xs, zs, shape, count))
    for n, (dx, dz) in enumerate(AROUND):
        adjoint_halos[n].wait_recv()
        ok = inside(-dx, -dz)
        if dz == 0:
            for f in range(2):
                a0e[f, land_x(dx, 4), OWN_Z, :] = bx[n, pl.ds(4 * f, 4)].astype(F32) * ok
        elif dx == 0:
            unpack_face(bz.at[n - 2], a0e, land_z(dz), ok)
        else:
            unpack_corner(bc.at[n - 4], a0e, [layer_at(dx, k, True) for k in (1, 2, 3)], land_z(dz), ok)

    start_sum(1, end_sum(0))

    def adjoint_part(t, _):
        for x in (HX - 3 + 2 * t, HX - 2 + 2 * t):
            for f in range(2):
                c, total = around(a0e, f, x)
                diag = 6.0 + LAPLACE_SHIFTS[f] * ce[x]
                w[f, x] = (diag * c - total) * mask[x]
                diagonal[f, x] = (diag - CENTRE[f]) * mask[x]
        return 0

    lax.fori_loop(0, CX // 2 + 3, adjoint_part, 0)

    pltpu.make_async_remote_copy(
        src_ref=cols.at[pl.ds(0, NB - 1)], dst_ref=cols.at[pl.ds(0, NB - 1)],
        send_sem=cols_sem.at[0], recv_sem=cols_sem.at[1],
        device_id=at(0, 1), device_id_type=MESH).wait_recv()
    cols[NB - 1] = aux[16:32, :]
    first_row = (d * ROWS).astype(F32)
    row_lane = iota((NNZ, 128), 1).astype(F32)

    def request(slot, _):
        row = 2.0 * cols[slot] - first_row
        hot = jnp.concatenate([jnp.where(row == row_lane, 1.0, 0.0), jnp.where(row + 1.0 == row_lane, 1.0, 0.0)], axis=0)
        pick_hot[pl.ds(pl.multiple_of(slot * 2 * NNZ, 2 * NNZ), 2 * NNZ)] = hot.astype(BF16)
        return 0

    lax.fori_loop(0, NB, request, 0)

    point_values.wait_recv()
    found = coefficients(end_sum(1))

    for n, (dx, dz) in enumerate(AROUND):
        xs, zs, shape, count = around_points[n]
        ok = inside(-dx, -dz)
        left = []
        for f in range(2):
            a = found[f]
            values = rseen[n, f:f + 1, :]
            for k in range(ITERS):
                values = values + a[k] * rseen[n, 2 * (k + 1) + f:2 * (k + 1) + f + 1, :]
            left.append((rec_hit[n, pl.ds(0, count)] * parts(values, ok)).astype(BF16))
        placed = lax.dot_general(jnp.concatenate(left, axis=0), rec_y[n], (((1,), (1,)), ((), ())),
                                 preferred_element_type=F32).reshape((2,) + shape + (NY,))
        v0[:, xs, zs, :] = placed - w[:, xs, zs, :]

    def own_residual(t, carry):
        for x in [HX + 8 * t + j for j in range(8)]:
            out = []
            for f in range(2):
                a = found[f]
                new = x0e[f, x, OWN_Z, :] + a[0] * v0[f, x, OWN_Z, :] + a[1] * v1[f, x, OWN_Z, :]
                new = new + a[2] * v2[f, x, OWN_Z, :]
                fwd[f, x - HX] = new
                u = cnte[x - HX] * new - obse[f, x - HX] - w[f, x, OWN_Z, :]
                v0[f, x, OWN_Z, :] = u
                p = u * u
                out.append(carry[f] + (p[0:8, 0:128] + p[8:16, 0:128]) + (p[0:8, 128:256] + p[8:16, 128:256]))
            carry = tuple(out)
        return carry

    squares = lax.fori_loop(0, CX // 8, own_residual, (jnp.zeros((8, 128), F32),) * 2)
    forward_store = pltpu.make_async_copy(fwd, fwd_out, out_sem.at[0])
    forward_store.start()

    sums = [squares] + krylov((2, 1), True)
    start_sum(2, pack_sums(sums))
    start_sum(3, end_sum(2))
    found_adjoint = coefficients(end_sum(3))

    def gradient_layer(x, _):
        total = jnp.zeros((CZ, NY), F32)
        for f in range(2):
            e = found_adjoint[f]
            own = a0e[f, x + HX, OWN_Z, :] + e[0] * v0[f, x + HX, OWN_Z, :] + e[1] * v1[f, x + HX, OWN_Z, :]
            own = own + e[2] * v2[f, x + HX, OWN_Z, :]
            total = total + LAPLACE_SHIFTS[f] * fwd[f, x] * own
        grad[pl.ds(x * CZ, CZ)] = (-total).astype(BF16)
        return 0

    for x in range(CX):
        gradient_layer(x, 0)

    psend[...] = jnp.dot(pick_hot[...], grad[...], preferred_element_type=F32).astype(BF16).reshape(NB, 2 * NNZ, NY)

    for i, step in enumerate(LAYERS):
        back = ((4 - step[0]) % 4,) + step[1:]
        pltpu.make_async_remote_copy(
            src_ref=psend.at[i], dst_ref=precv.at[i], send_sem=pick_sem.at[0], recv_sem=pick_sem.at[1],
            device_id=beside(back), device_id_type=MESH).start()

    cov_load.wait()
    picks = pltpu.make_async_remote_copy(
        src_ref=precv, dst_ref=precv, send_sem=pick_sem.at[0], recv_sem=pick_sem.at[1],
        device_id=at(0, 1), device_id_type=MESH)
    picks.wait_recv()
    picked = psend[NB - 1]
    for i in range(NB - 1):
        picked = picked + precv[i]

    term_row = iota((NNZ, BLOCK), 0)

    def term(t, total):
        for k in range(NNZ):
            block = cov[k]
            made = lax.dot_general(picked[0:NNZ], block[:, 0:NY], (((1,), (1,)), ((), ())), preferred_element_type=F32)
            made += lax.dot_general(picked[NNZ:], block[:, NY:], (((1,), (1,)), ((), ())), preferred_element_type=F32)
            total = jnp.where(term_row == k, made, total)
        return total

    terms = lax.fori_loop(0, 1, term, jnp.zeros((NNZ, BLOCK), F32))
    cov_rows = rows_v[0].astype(F32)
    out_row = iota((ROWS, NNZ), 0).astype(F32)
    total = grad[...].astype(F32)
    for half in range(2):
        hot = jnp.where(2.0 * cov_rows + float(half) == out_row, 1.0, 0.0)
        total = total + jnp.dot(hot, terms[:, half * NY:(half + 1) * NY], precision=lax.Precision.HIGHEST,
                                preferred_element_type=F32)
    pre[...] = total.reshape(CX, CZ, NY)
    pre_store = pltpu.make_async_copy(pre, pre_out, out_sem.at[1])
    pre_store.start()

    lists.wait_send()
    for copy in halos + adjoint_halos + [point_values]:
        copy.wait_send()
    pltpu.make_async_remote_copy(
        src_ref=cols.at[pl.ds(0, NB - 1)], dst_ref=cols.at[pl.ds(0, NB - 1)],
        send_sem=cols_sem.at[0], recv_sem=cols_sem.at[1],
        device_id=at(0, 1), device_id_type=MESH).wait_send()
    for stage in range(4):
        pltpu.make_async_remote_copy(
            src_ref=rsum.at[stage], dst_ref=rsum.at[stage],
            send_sem=sum_sem.at[stage, 0], recv_sem=sum_sem.at[stage, 1],
            device_id=at(0, 1), device_id_type=MESH).wait_send()
    picks.wait_send()
    forward_store.wait()
    pre_store.wait()


def hand_over(fwd_in, pre_in, fwd_out, pre_out):
    fwd_out[...] = fwd_in[...]
    pre_out[...] = pre_in[...]


def local(conductivity, initial_field, adjoint_initial, src_cell, src_amp, rec_cell, observed, cov_blocks, cov_rows, cov_cols):
    big = pltpu.VMEM((2, EX, EZ, NY), F32)
    one = pltpu.VMEM((EX, EZ, NY), F32)
    dma = pltpu.SemaphoreType.DMA
    scratch = [
        pltpu.VMEM(src_cell.shape, jnp.int32), pltpu.VMEM(src_amp.shape, F32),
        pltpu.VMEM(rec_cell.shape, jnp.int32), pltpu.VMEM(observed.shape, F32),
        pltpu.VMEM(cov_rows.shape, jnp.int32), pltpu.VMEM(cov_cols.shape, jnp.int32),
        pltpu.VMEM((32, 128), F32), pltpu.VMEM((NNZ, BLOCK, BLOCK), BF16),
        one, big, big, one, big,
        pltpu.VMEM((2, CX, CZ, NY), F32), pltpu.VMEM((CX, CZ, NY), F32),
        big, big, big, big, big,
        pltpu.VMEM((2, CX, CZ, NY), F32), pltpu.VMEM((ROWS, NY), BF16), pltpu.VMEM((CX, CZ, NY), F32),
        pltpu.VMEM((2 * NNZ * NB, ROWS), BF16),
    ]
    for count, slabs in ((2, 11), (2, 6), (4, 2), (2, 8), (2, 4), (4, 2)):
        scratch += [pltpu.VMEM((count, slabs, 16, NY), BF16)] * 2
    scratch += [
        pltpu.VMEM((8, 16, 128), F32), pltpu.VMEM((8, 128), F32), pltpu.VMEM((8, 8, 128), F32),
        pltpu.VMEM((8, 64, 128), F32), pltpu.VMEM((8, NY, 128), BF16), pltpu.VMEM((NB, NNZ, 128), F32),
        pltpu.VMEM((4, 8, 128), F32), pltpu.VMEM((4, NB - 1, 8, 128), F32),
        pltpu.VMEM((NB, 2 * NNZ, NY), BF16), pltpu.VMEM((NB - 1, 2 * NNZ, NY), BF16),
        dma((9,)), dma, dma((2,)), dma((2,)), dma((2,)), dma((8, 2)), dma((8, 2)), dma((2,)), dma((4, 2)), dma((2,)),
    ]
    anywhere = pl.BlockSpec(memory_space=pl.ANY)
    results = pl.pallas_call(
        kernel,
        out_shape=(
            jax.ShapeDtypeStruct((2, CX, CZ, NY), F32),
            jax.ShapeDtypeStruct((CX, CZ, NY), F32),
        ),
        in_specs=[anywhere] * 10,
        out_specs=(anywhere, anywhere),
        scratch_shapes=scratch,
        compiler_params=pltpu.CompilerParams(
            collective_id=0, has_side_effects=True, vmem_limit_bytes=56 * 2**20),
    )(conductivity, initial_field, adjoint_initial, src_cell, src_amp, rec_cell, observed,
      cov_blocks.reshape(NNZ, BLOCK, BLOCK), cov_rows, cov_cols)
    return pl.pallas_call(
        hand_over,
        out_shape=[jax.ShapeDtypeStruct(r.shape, r.dtype) for r in results],
    )(*results)


def solution(mesh):
    return jax.shard_map(
        local,
        mesh=mesh,
        in_specs=(
            P("brick", "depth", None),
            P(None, "brick", "depth", None),
            P(None, "brick", "depth", None),
            P("brick", "depth", None),
            P("brick", "depth", None, None),
            P("brick", "depth", None),
            P("brick", "depth", None, None),
            P("brick", "depth", None, None, None),
            P("brick", "depth", None),
            P("brick", "depth", None),
        ),
        out_specs=(P(None, "brick", "depth", None), P("brick", "depth", None)),
        check_vma=False,
    )
```
